32 devices in a mesh: neuron: 8 (over z, y), trial: 4 (over x, core).
Axes of the slice: x: 2, y: 2, z: 4, core: 2. Of those that a mesh axis runs over, the one named last changes fastest.
Arguments:
- tensor: bfloat16 [8, 1024, 1024], P('trial', 'neuron'), may hold values from -1000 to 1000
- time_init: float32 [32, 1024], replicated, may hold values from -6 to 6
- trial_init: float32 [32, 8], P(None, 'trial'), may hold values from -6 to 6
Outputs:
- neuron_factor: float32 [32, 1024], P(None, 'neuron')
- time_factor: float32 [32, 1024], P(None, ('neuron', 'trial'))
- trial_factor: float32 [32, 8], P(None, 'trial')
The draws below stay inside these ranges and needn't reach their ends.
All inputs are finite; a program needn't handle non-finite values.
Results may differ from the reference program's by a relative error of at most 0.011.
Values may be sent and summed in bfloat16 or wider, within the bound.
A program may use at most 64 MiB of HBM per device.

```python
import math
import jax
import jax.numpy as jnp
from jax import lax

TIMEPOINTS = 1024
COMPONENTS = 32
SWEEPS = 2
NEURONS = 1024
TRIALS = 8


def draw_tensor(key, part):
    key_list = jax.random.split(jax.random.fold_in(key, 11), 6)
    neuron_part = jax.random.truncated_normal(key_list[0], -4.0, 4.0, (COMPONENTS, NEURONS), jnp.float32)
    time_part = jax.random.truncated_normal(key_list[1], -4.0, 4.0, (COMPONENTS, TIMEPOINTS), jnp.float32)
    trial_part = jax.random.truncated_normal(key_list[2], -4.0, 4.0, (COMPONENTS, TRIALS), jnp.float32)
    strength = jnp.exp(jax.random.uniform(key_list[3], (COMPONENTS,), jnp.float32, math.log(0.3), math.log(3.0)))
    places = jnp.arange(NEURONS, dtype=jnp.float32) / NEURONS
    spread = jnp.exp(jax.random.uniform(key_list[4], (NEURONS,), jnp.float32, 0.0, math.log(10.0)))
    ramp_up = jnp.exp(0.5 * math.log(3.0) * places)
    row_scale = spread * ramp_up / 4.0

    def one_trial(trial_index):
        noise_key = jax.random.fold_in(key_list[5], trial_index)
        noise_part = jax.random.truncated_normal(noise_key, -4.0, 4.0, (NEURONS, TIMEPOINTS), jnp.float32)
        mixing = trial_part[:, trial_index] * strength / math.sqrt(COMPONENTS)
        signal = lax.dot_general(neuron_part * mixing[:, None], time_part, (((0,), (0,)), ((), ())), precision=lax.Precision.HIGHEST, preferred_element_type=jnp.float32)
        return (row_scale[:, None] * (signal + 0.7 * noise_part)).astype(jnp.bfloat16)
    return lax.map(one_trial, jnp.arange(TRIALS, dtype=jnp.int32))


def level_of(own_key, shape, cuts, least, top_value):
    def one(dim, blocks):
        steps = jax.random.uniform(jax.random.fold_in(jax.random.fold_in(own_key, 6), dim), (blocks,), jnp.float32, least / len(cuts), top_value / len(cuts))
        return jnp.repeat(jnp.exp(steps), shape[dim] // blocks).reshape((-1,) + (1,) * (len(shape) - dim - 1))

    loudness = one(*cuts[0])
    for cut in cuts[1:]:
        loudness = loudness * one(*cut)
    return loudness


def normal_values(rng, dims, deviation, reach, cuts=(), kind=jnp.bfloat16):
    factor_of = level_of(rng, dims, cuts, -0.22, 0.18) if cuts else 1.0
    values = jax.random.normal(rng, dims, jnp.float32) * deviation * factor_of
    return jnp.minimum(jnp.maximum(values, -reach), reach).astype(kind)


def setup_inputs(seed: int = 0) -> dict:
    keys = jax.random.split(jax.random.key(seed), 4)
    return {
        "tensor": draw_tensor(jax.random.fold_in(keys[3], 71), 0),
        "time_init": normal_values(keys[1], (COMPONENTS, TIMEPOINTS), 1.0, 6.0, (), jnp.float32),
        "trial_init": normal_values(keys[2], (COMPONENTS, TRIALS), 1.0, 6.0, ((1, 4),), jnp.float32),
    }


ridge_share = 0.1
tiny_eps = 1e-06

def gram_of(matrix):
    return lax.dot_general(matrix.astype(jnp.float32), matrix.astype(jnp.float32), (((1,), (1,)), ((), ())), precision=lax.Precision.HIGHEST, preferred_element_type=jnp.float32)

def damped_solve(gram_mat, right_hand):
    order_size = gram_mat.shape[0]
    identity_mat = jnp.eye(order_size, dtype=jnp.float32)
    damped = gram_mat + ridge_share * (jnp.trace(gram_mat) / order_size) * identity_mat
    cholesky_low = jnp.linalg.cholesky(damped)
    return jax.scipy.linalg.cho_solve((cholesky_low, True), right_hand)

def reference(tensor, time_init, trial_init):
    time_now = time_init
    trial_now = trial_init
    neuron_now = jnp.zeros((time_init.shape[0], tensor.shape[1]), jnp.float32)
    for sweep_index in range(SWEEPS):
        time_rounded = time_now.astype(jnp.bfloat16)

        def project_one(trial_slab):
            return lax.dot_general(time_rounded.astype(jnp.float32), trial_slab.astype(jnp.float32), (((1,), (1,)), ((), ())), preferred_element_type=jnp.float32)
        projected = lax.map(project_one, tensor)
        time_gram = gram_of(time_now)
        trial_gram = gram_of(trial_now)
        neuron_terms = lax.optimization_barrier(jnp.sum(trial_now.T[:, :, None] * projected, axis=0))
        neuron_raw = damped_solve(trial_gram * time_gram, neuron_terms)
        neuron_now = neuron_raw / jnp.sqrt(lax.optimization_barrier(jnp.mean(neuron_raw * neuron_raw, axis=1, keepdims=True)) + tiny_eps)
        neuron_gram = gram_of(neuron_now)
        trial_terms = lax.optimization_barrier(jnp.sum(neuron_now[None] * projected, axis=2)).T
        trial_now = damped_solve(neuron_gram * time_gram, trial_terms)
        trial_gram = gram_of(trial_now)
        weights = (neuron_now[None] * trial_now.T[:, :, None]).astype(jnp.bfloat16)

        def accumulate(running, paired):
            return (running + jnp.dot(paired[0].astype(jnp.float32), paired[1].astype(jnp.float32), preferred_element_type=jnp.float32), None)
        time_terms, unused = lax.scan(accumulate, jnp.zeros(time_now.shape, jnp.float32), (weights, tensor))
        time_raw = damped_solve(neuron_gram * trial_gram, time_terms)
        time_now = time_raw / jnp.sqrt(lax.optimization_barrier(jnp.mean(time_raw * time_raw, axis=1, keepdims=True)) + tiny_eps)
    return (neuron_now, time_now, trial_now)
```

```python
import functools

import jax
import jax.numpy as jnp
from jax import lax
from jax.experimental import pallas as pl
from jax.experimental.pallas import tpu as pltpu
from jax.sharding import PartitionSpec as P

SWEEPS = 2

ridge_share = 0.1
tiny_eps = 1e-06
LANES = 128
ROWS = 8
MESH = pl.DeviceIdType.MESH
EXACT = lax.Precision.HIGHEST
NT = (((1,), (1,)), ((), ()))


def each(low, high, step):
    if high - low <= 40:
        for index in range(low, high):
            step(index)
    else:

        def body(index, carry):
            step(index)
            return carry

        lax.fori_loop(low, high, body, 0)


def wait_bytes(ref, sem):
    pltpu.make_async_copy(ref, ref, sem).wait()


def kernel(
    neuron_devices,
    trial_devices,
    tensor_hbm,
    time_ref,
    trial_ref,
    neuron_out,
    time_out,
    trial_out,
    tensor_v,
    trial_all,
    proj_all,
    gram_all,
    time_local,
    time_parts,
    time_sums,
    time_keep,
    load_sem,
    trial_sem,
    send_sem,
    recv_sem,
):
    trials_here, neurons_here, timepoints = tensor_hbm.shape
    comps = time_ref.shape[0]
    devices = neuron_devices * trial_devices
    trials = trials_here * trial_devices
    neurons = neurons_here * neuron_devices
    chunks = timepoints // LANES
    groups = comps // ROWS
    tiles = chunks * groups
    units = min(devices, tiles)
    per = tiles // units
    stride = devices // units
    my_neuron = lax.axis_index("neuron")
    my_trial = lax.axis_index("trial")
    me = my_neuron * trial_devices + my_trial

    def device_of(linear):
        return (linear // trial_devices, lax.rem(linear, trial_devices))

    loads = []
    for k in range(trials_here):
        load = pltpu.make_async_copy(
            tensor_hbm.at[k],
            tensor_v.at[pl.ds(k * neurons_here, neurons_here)],
            load_sem.at[k],
        )
        load.start()
        loads.append(load)

    barrier = pltpu.get_barrier_semaphore()

    def greet(step):
        pl.semaphore_signal(
            barrier,
            inc=1,
            device_id=device_of(lax.rem(me + step, devices)),
            device_id_type=MESH,
        )

    each(1, devices, greet)

    lane = lax.broadcasted_iota(jnp.int32, (comps, LANES), 1)
    row = lax.broadcasted_iota(jnp.int32, (comps, LANES), 0)
    eye = (lane == row).astype(jnp.float32)
    right_eye = (lane == row + comps).astype(jnp.float32)
    in_gram = lane < comps
    in_right = (lane >= comps) & (lane < 2 * comps)
    in_terms = (lane >= comps) & (lane < comps + trials)

    def wide_gram(matrix):
        padded = jnp.concatenate(
            [matrix, jnp.zeros((LANES - comps, matrix.shape[1]), matrix.dtype)], axis=0
        )
        return lax.dot_general(
            matrix, padded, NT, precision=EXACT, preferred_element_type=jnp.float32
        )

    def eliminate(system):
        for k in range(0, comps, 2):
            col0 = jnp.broadcast_to(system[:, k : k + 1], (comps, LANES))
            col1 = jnp.broadcast_to(system[:, k + 1 : k + 2], (comps, LANES))
            row0 = system[k : k + 1, :]
            row1 = system[k + 1 : k + 2, :]
            a, c = col0[k : k + 1, :], col0[k + 1 : k + 2, :]
            b, d = col1[k : k + 1, :], col1[k + 1 : k + 2, :]
            inverse = 1.0 / (a * d - b * c)
            new0 = (d * row0 - b * row1) * inverse
            new1 = (a * row1 - c * row0) * inverse
            system = system - col0 * new0 - col1 * new1
            system = jnp.where(row == k, new0, jnp.where(row == k + 1, new1, system))
        return system

    def mean_trace(gram):
        return jnp.sum(
            jnp.sum(gram * eye, axis=0, keepdims=True), axis=1, keepdims=True
        ) * (1.0 / comps)

    def inverse_of(gram):
        scale = 1.0 / mean_trace(gram)
        system = eliminate((gram * scale + ridge_share * eye) + right_eye * scale)
        return jnp.where(in_right, system, 0.0)

    def apply_inverse(inverse, right_hand):
        width = right_hand.shape[1]
        padded = jnp.concatenate(
            [
                jnp.zeros((comps, width), jnp.float32),
                right_hand,
                jnp.zeros((LANES - 2 * comps, width), jnp.float32),
            ],
            axis=0,
        )
        return lax.dot_general(
            inverse,
            padded,
            (((1,), (0,)), ((), ())),
            precision=EXACT,
            preferred_element_type=jnp.float32,
        )

    def send_all(source, target, count, target_of, sends, receives):
        def start(step):
            pltpu.make_async_remote_copy(
                src_ref=source,
                dst_ref=target,
                send_sem=sends,
                recv_sem=receives,
                device_id=target_of(step),
                device_id_type=MESH,
            ).start()

        each(1, count, start)

    def trial_peer(step):
        return (my_neuron, lax.rem(my_trial + step, trial_devices))

    def neuron_peer(step):
        return (lax.rem(my_neuron + step, neuron_devices), my_trial)

    time_now = time_ref[...]
    time_rounded = time_now.astype(jnp.bfloat16)
    time_gram = wide_gram(time_now)
    placed = jnp.zeros((comps, LANES), jnp.float32)
    for k in range(trials_here):
        placed = jnp.where(
            lane == comps + my_trial * trials_here + k, trial_ref[:, k : k + 1], placed
        )
    trial_all[0] = placed

    pl.semaphore_wait(barrier, devices - 1)

    def start_trial(step):
        pltpu.make_async_remote_copy(
            src_ref=trial_all.at[0],
            dst_ref=trial_all.at[step],
            send_sem=trial_sem.at[0],
            recv_sem=trial_sem.at[1],
            device_id=trial_peer(step),
            device_id_type=MESH,
        ).start()

    each(1, trial_devices, start_trial)
    for load in loads:
        load.wait()

    trial_wide = None
    trial_gram = None
    for sweep in range(SWEEPS):
        sends = [send_sem.at[sweep, phase] for phase in range(4)]
        receives = [recv_sem.at[sweep, phase] for phase in range(4)]

        projected = lax.dot_general(
            time_rounded, tensor_v[...], NT, preferred_element_type=jnp.float32
        )
        for k in range(trials_here):
            proj_all[sweep, my_trial, k] = projected[
                :, k * neurons_here : (k + 1) * neurons_here
            ]
        mine = proj_all.at[sweep, my_trial]
        send_all(mine, mine, trial_devices, trial_peer, sends[0], receives[0])
        if sweep == 0:
            others = trial_all.at[pl.ds(1, trial_devices - 1)]
            wait_bytes(others, trial_sem.at[1])
            wait_bytes(others, trial_sem.at[0])
            trial_wide = jnp.sum(trial_all[...], axis=0)
            trial_gram = wide_gram(trial_wide)
        inverse = inverse_of(trial_gram * time_gram)
        others = proj_all.at[sweep, pl.ds(0, trial_devices - 1)]
        wait_bytes(others, receives[0])

        blocks = [
            proj_all[sweep, k // trials_here, k % trials_here] for k in range(trials)
        ]
        terms = jnp.zeros((comps, neurons_here), jnp.float32)
        for k in range(trials):
            terms = terms + trial_wide[:, comps + k : comps + k + 1] * blocks[k]
        neuron_raw = apply_inverse(inverse, terms)
        payload = wide_gram(neuron_raw)
        for k in range(trials):
            total = jnp.sum(neuron_raw * blocks[k], axis=1, keepdims=True)
            payload = jnp.where(lane == comps + k, total, payload)
        half = comps // 2
        folded = payload[:half] + pltpu.roll(payload[half:], LANES // 2, 1)
        gram_all[sweep, 0] = folded

        def start_gram(step):
            pltpu.make_async_remote_copy(
                src_ref=gram_all.at[sweep, 0],
                dst_ref=gram_all.at[sweep, step],
                send_sem=sends[1],
                recv_sem=receives[1],
                device_id=neuron_peer(step),
                device_id_type=MESH,
            ).start()

        each(1, neuron_devices, start_gram)
        wait_bytes(others, sends[0])
        others = gram_all.at[sweep, pl.ds(1, neuron_devices - 1)]
        wait_bytes(others, receives[1])
        folded = jnp.sum(gram_all[sweep], axis=0)
        payload = jnp.concatenate([folded, pltpu.roll(folded, LANES // 2, 1)], axis=0)
        raw_gram = jnp.where(in_gram, payload, 0.0)

        squares = raw_gram * eye
        down = lax.rsqrt(
            jnp.sum(squares, axis=1, keepdims=True) * (1.0 / neurons) + tiny_eps
        )
        across = lax.rsqrt(
            jnp.sum(squares, axis=0, keepdims=True) * (1.0 / neurons) + tiny_eps
        )
        neuron_now = neuron_raw * down
        neuron_gram = raw_gram * down * across
        gram = neuron_gram * time_gram
        scale = 1.0 / mean_trace(gram)
        system = jnp.where(
            in_gram,
            gram * scale + ridge_share * eye,
            jnp.where(in_terms, payload * down * scale, 0.0),
        )
        system = eliminate(system)
        trial_wide = jnp.where(in_terms, system, 0.0)
        own = [
            jnp.sum(
                jnp.where(
                    lane == comps + my_trial * trials_here + k, trial_wide, 0.0
                ),
                axis=1,
                keepdims=True,
            )
            for k in range(trials_here)
        ]

        weights = jnp.concatenate(
            [(neuron_now * own[k]).astype(jnp.bfloat16) for k in range(trials_here)],
            axis=1,
        )
        local = jnp.dot(weights, tensor_v[...], preferred_element_type=jnp.float32)
        for c in range(chunks):
            for g in range(groups):
                time_local[sweep, c * groups + g] = local[
                    g * ROWS : (g + 1) * ROWS, c * LANES : (c + 1) * LANES
                ]
        my_unit = me // stride

        def start_part(step):
            unit = lax.rem(my_unit + step, units)
            owner = unit * stride
            slot = lax.rem(owner - me + devices, devices)
            pltpu.make_async_remote_copy(
                src_ref=time_local.at[sweep, pl.ds(unit * per, per)],
                dst_ref=time_parts.at[sweep, slot],
                send_sem=sends[2],
                recv_sem=receives[2],
                device_id=device_of(owner),
                device_id_type=MESH,
            ).start()

        each(1, units, start_part)
        if stride > 1:
            pl.when(lax.rem(me, stride) != 0)(lambda: start_part(0))
        trial_gram = wide_gram(trial_wide)
        inverse = inverse_of(neuron_gram * trial_gram)
        wait_bytes(others, sends[1])

        def reduce_and_send():
            wait_bytes(time_parts.at[sweep, pl.ds(1, devices - 1)], receives[2])
            slice_here = pl.ds(my_unit * per, per)
            total = time_local[sweep, slice_here]
            total = total + jnp.sum(time_parts[sweep, pl.ds(1, devices - 1)], axis=0)
            time_sums[sweep, slice_here] = total
            mine = time_sums.at[sweep, slice_here]

            def start_sum(step):
                pltpu.make_async_remote_copy(
                    src_ref=mine,
                    dst_ref=mine,
                    send_sem=sends[3],
                    recv_sem=receives[3],
                    device_id=device_of(lax.rem(me + step, devices)),
                    device_id_type=MESH,
                ).start()

            each(1, devices, start_sum)
            some = time_sums.at[sweep, pl.ds(0, (units - 1) * per)]
            wait_bytes(some, receives[3])
            wait_bytes(some, sends[2])
            wait_bytes(time_parts.at[sweep, pl.ds(1, devices - 1)], sends[3])

        def send_only():
            wait_bytes(time_sums.at[sweep], receives[3])
            wait_bytes(time_sums.at[sweep], sends[2])

        if stride == 1:
            reduce_and_send()
        else:
            pl.when(lax.rem(me, stride) == 0)(reduce_and_send)
            pl.when(lax.rem(me, stride) != 0)(send_only)
        time_terms = jnp.concatenate(
            [
                time_sums[sweep, pl.ds(c * groups, groups)].reshape(comps, LANES)
                for c in range(chunks)
            ],
            axis=1,
        )
        time_raw = apply_inverse(inverse, time_terms)
        if sweep < SWEEPS - 1:
            raw_gram = wide_gram(time_raw)
            squares = raw_gram * eye
            down = lax.rsqrt(
                jnp.sum(squares, axis=1, keepdims=True) * (1.0 / timepoints) + tiny_eps
            )
            across = lax.rsqrt(
                jnp.sum(squares, axis=0, keepdims=True) * (1.0 / timepoints) + tiny_eps
            )
            time_gram = raw_gram * down * across
            time_rounded = (time_raw * down).astype(jnp.bfloat16)
        else:
            down = lax.rsqrt(
                jnp.sum(time_raw * time_raw, axis=1, keepdims=True)
                * (1.0 / timepoints)
                + tiny_eps
            )
            for c in range(chunks):
                time_keep[c] = time_raw[:, c * LANES : (c + 1) * LANES] * down
            share = timepoints // devices
            shares = LANES // share
            chunk = time_keep[me // shares]
            shift = lax.rem(LANES - lax.rem(me, shares) * share, LANES)
            time_out[...] = pltpu.roll(chunk, shift, 1)[:, :share]
            neuron_out[...] = neuron_now
            for k in range(trials_here):
                trial_out[:, k : k + 1] = own[k]


def per_device(neuron_devices, trial_devices, tensor, time_init, trial_init):
    trials_here, neurons_here, timepoints = tensor.shape
    comps = time_init.shape[0]
    devices = neuron_devices * trial_devices
    tiles = (timepoints // LANES) * (comps // ROWS)
    per = tiles // min(devices, tiles)
    f32 = jnp.float32
    vmem = pl.BlockSpec(memory_space=pltpu.VMEM)
    return pl.pallas_call(
        functools.partial(kernel, neuron_devices, trial_devices),
        out_shape=(
            jax.ShapeDtypeStruct((comps, neurons_here), f32),
            jax.ShapeDtypeStruct((comps, timepoints // devices), f32),
            jax.ShapeDtypeStruct((comps, trials_here), f32),
        ),
        in_specs=[pl.BlockSpec(memory_space=pl.ANY), vmem, vmem],
        out_specs=(vmem, vmem, vmem),
        scratch_shapes=[
            pltpu.VMEM((trials_here * neurons_here, timepoints), jnp.bfloat16),
            pltpu.VMEM((trial_devices, comps, LANES), f32),
            pltpu.VMEM((SWEEPS, trial_devices, trials_here, comps, neurons_here), f32),
            pltpu.VMEM((SWEEPS, neuron_devices, comps // 2, LANES), f32),
            pltpu.VMEM((SWEEPS, tiles, ROWS, LANES), f32),
            pltpu.VMEM((SWEEPS, devices, per, ROWS, LANES), f32),
            pltpu.VMEM((SWEEPS, tiles, ROWS, LANES), f32),
            pltpu.VMEM((timepoints // LANES, comps, LANES), f32),
            pltpu.SemaphoreType.DMA((trials_here,)),
            pltpu.SemaphoreType.DMA((2,)),
            pltpu.SemaphoreType.DMA((SWEEPS, 4)),
            pltpu.SemaphoreType.DMA((SWEEPS, 4)),
        ],
        compiler_params=pltpu.CompilerParams(
            collective_id=0,
            has_side_effects=True,
            vmem_limit_bytes=32 * 1024 * 1024,
        ),
    )(tensor, time_init, trial_init)


def solution(mesh):
    placed = (P("trial", "neuron", None), P(), P(None, "trial"))
    return jax.shard_map(
        functools.partial(per_device, mesh.shape["neuron"], mesh.shape["trial"]),
        mesh=mesh,
        in_specs=placed,
        out_specs=(P(None, "neuron"), P(None, ("neuron", "trial")), P(None, "trial")),
        check_vma=False,
    )
```

```python
import functools

import jax
import jax.numpy as jnp
from jax import lax
from jax.experimental import pallas as pl
from jax.experimental.pallas import tpu as pltpu
from jax.sharding import PartitionSpec as P

SWEEPS = 2

ridge_share = 0.1
tiny_eps = 1e-06
LANES = 128
ROWS = 8
MESH = pl.DeviceIdType.MESH
EXACT = lax.Precision.HIGHEST
NT = (((1,), (1,)), ((), ()))


def each(low, high, step):
    if high - low <= 40:
        for index in range(low, high):
            step(index)
    else:

        def body(index, carry):
            step(index)
            return carry

        lax.fori_loop(low, high, body, 0)


def wait_bytes(ref, sem):
    pltpu.make_async_copy(ref, ref, sem).wait()


def kernel(
    neuron_devices,
    trial_devices,
    tensor_hbm,
    time_hbm,
    trial_hbm,
    neuron_out,
    time_out,
    trial_out,
    tensor_v,
    time_ref,
    trial_ref,
    trial_all,
    proj_all,
    gram_all,
    time_local,
    time_parts,
    time_sums,
    time_keep,
    norm_all,
    load_sem,
    norm_sem,
    trial_sem,
    send_sem,
    recv_sem,
):
    trials_here, neurons_here, timepoints = tensor_hbm.shape
    comps = time_hbm.shape[0]
    devices = neuron_devices * trial_devices
    trials = trials_here * trial_devices
    neurons = neurons_here * neuron_devices
    chunks = timepoints // LANES
    groups = comps // ROWS
    tiles = chunks * groups
    units = min(devices, tiles)
    per = tiles // units
    stride = devices // units
    my_neuron = lax.axis_index("neuron")
    my_trial = lax.axis_index("trial")
    me = my_neuron * trial_devices + my_trial

    direct = stride == 1 and devices <= 64
    share = timepoints // devices
    by_columns = direct and share * groups == LANES
    neuron_ids = [
        lax.rem(my_neuron + step, neuron_devices)
        for step in range(neuron_devices if direct else 0)
    ]
    trial_ids = [lax.rem(my_trial + step, trial_devices) for step in range(trial_devices)]

    def device_of(linear):
        return (linear // trial_devices, lax.rem(linear, trial_devices))

    def each_other(visit):
        if direct:
            for slot in range(1, devices):
                visit(
                    slot,
                    (
                        neuron_ids[slot // trial_devices],
                        trial_ids[slot % trial_devices],
                    ),
                )
        else:
            each(
                1,
                devices,
                lambda step: visit(step, device_of(lax.rem(me + step, devices))),
            )

    time_load = pltpu.make_async_copy(time_hbm, time_ref, load_sem.at[0])
    time_load.start()
    trial_load = pltpu.make_async_copy(trial_hbm, trial_ref, load_sem.at[1])
    trial_load.start()
    loads = []
    for k in range(trials_here):
        load = pltpu.make_async_copy(
            tensor_hbm.at[k],
            tensor_v.at[pl.ds(k * neurons_here, neurons_here)],
            load_sem.at[2 + k],
        )
        load.start()
        loads.append(load)

    barrier = pltpu.get_barrier_semaphore()

    def greet(slot, device):
        pl.semaphore_signal(barrier, inc=1, device_id=device, device_id_type=MESH)

    each_other(greet)

    lane = lax.broadcasted_iota(jnp.int32, (comps, LANES), 1)
    row = lax.broadcasted_iota(jnp.int32, (comps, LANES), 0)
    eye = (lane == row).astype(jnp.float32)
    right_eye = ((lane >= comps) & (lax.rem(lane, comps) == row)).astype(jnp.float32)
    in_gram = lane < comps
    lane8 = lax.broadcasted_iota(jnp.int32, (ROWS, LANES), 1)
    in_low = (lane >= 2 * comps) & (lane < 3 * comps)
    in_terms = (lane >= comps) & (lane < comps + trials)

    def wide_gram(matrix):
        padded = jnp.concatenate(
            [matrix, jnp.zeros((LANES - comps, matrix.shape[1]), matrix.dtype)], axis=0
        )
        return lax.dot_general(
            matrix, padded, NT, precision=EXACT, preferred_element_type=jnp.float32
        )

    def split(matrix):
        high = matrix.astype(jnp.bfloat16)
        return high, (matrix - high.astype(jnp.float32)).astype(jnp.bfloat16)

    def split_gram(matrix):
        high, low = split(matrix)
        left = jnp.concatenate([high, low, high], axis=1)
        right = jnp.concatenate([high, high, low], axis=1)
        blank = jnp.zeros((LANES - comps, right.shape[1]), jnp.bfloat16)
        return lax.dot_general(
            left,
            jnp.concatenate([right, blank], axis=0),
            NT,
            preferred_element_type=jnp.float32,
        )

    def eliminate(system):
        for k in range(0, comps, 4):
            cols = [
                jnp.broadcast_to(system[:, k + j : k + j + 1], (comps, LANES))
                for j in range(4)
            ]
            for pair in (0, 2):
                top, low = k + pair, k + pair + 1
                col0, col1 = cols[pair], cols[pair + 1]
                a, c = col0[top : top + 1, :], col0[low : low + 1, :]
                b, d = col1[top : top + 1, :], col1[low : low + 1, :]
                inverse = 1.0 / (a * d - b * c)
                a, b, c, d = a * inverse, b * inverse, c * inverse, d * inverse

                def step(matrix):
                    row0, row1 = matrix[top : top + 1, :], matrix[low : low + 1, :]
                    new0 = d * row0 - b * row1
                    new1 = a * row1 - c * row0
                    matrix = matrix - col0 * new0 - col1 * new1
                    return jnp.where(
                        row == top, new0, jnp.where(row == low, new1, matrix)
                    )

                if pair == 0:
                    cols[2], cols[3] = step(cols[2]), step(cols[3])
                system = step(system)
        return system

    def mean_trace(gram):
        return jnp.sum(
            jnp.sum(gram * eye, axis=0, keepdims=True), axis=1, keepdims=True
        ) * (1.0 / comps)

    def inverse_of(gram):
        scale = 1.0 / mean_trace(gram)
        system = eliminate((gram * scale + ridge_share * eye) + right_eye * scale)
        low = system - system.astype(jnp.bfloat16).astype(jnp.float32)
        return jnp.where(in_gram, 0.0, jnp.where(in_low, low, system)).astype(
            jnp.bfloat16
        )

    def apply_inverse(inverse, right_hand):
        width = right_hand.shape[1]
        high, low = split(right_hand)
        padded = jnp.concatenate(
            [jnp.zeros((comps, width), jnp.bfloat16), high, high, low], axis=0
        )
        return lax.dot_general(
            inverse,
            padded,
            (((1,), (0,)), ((), ())),
            preferred_element_type=jnp.float32,
        )

    def send_all(source, target, count, target_of, sends, receives):
        def start(step):
            pltpu.make_async_remote_copy(
                src_ref=source,
                dst_ref=target,
                send_sem=sends,
                recv_sem=receives,
                device_id=target_of(step),
                device_id_type=MESH,
            ).start()

        each(1, count, start)

    def trial_peer(step):
        return (my_neuron, trial_ids[step])

    def neuron_peer(step):
        if direct:
            return (neuron_ids[step], my_trial)
        return (lax.rem(my_neuron + step, neuron_devices), my_trial)

    trial_load.wait()
    placed = jnp.zeros((comps, LANES), jnp.float32)
    for k in range(trials_here):
        column = jnp.sum(
            trial_ref[k : k + 1, :] * eye[:, :comps], axis=1, keepdims=True
        )
        placed = jnp.where(
            lane == comps + my_trial * trials_here + k, column, placed
        )
    trial_all[0] = placed
    time_load.wait()
    time_now = time_ref[...]
    time_rounded = time_now.astype(jnp.bfloat16)

    pl.semaphore_wait(barrier, devices - 1)

    def start_trial(step):
        pltpu.make_async_remote_copy(
            src_ref=trial_all.at[0],
            dst_ref=trial_all.at[step],
            send_sem=trial_sem.at[0],
            recv_sem=trial_sem.at[1],
            device_id=trial_peer(step),
            device_id_type=MESH,
        ).start()

    each(1, trial_devices, start_trial)
    for load in loads:
        load.wait()

    trial_wide = None
    trial_gram = None
    for sweep in range(SWEEPS):
        sends = [send_sem.at[sweep, phase] for phase in range(4)]
        receives = [recv_sem.at[sweep, phase] for phase in range(4)]

        projected = lax.dot_general(
            time_rounded, tensor_v[...], NT, preferred_element_type=jnp.float32
        )
        for k in range(trials_here):
            proj_all[sweep, my_trial, k] = projected[
                :, k * neurons_here : (k + 1) * neurons_here
            ]
        mine = proj_all.at[sweep, my_trial]
        send_all(mine, mine, trial_devices, trial_peer, sends[0], receives[0])
        time_gram = split_gram(time_now)
        if sweep == 0:
            others = trial_all.at[pl.ds(1, trial_devices - 1)]
            wait_bytes(others, trial_sem.at[1])
            wait_bytes(others, trial_sem.at[0])
            trial_wide = jnp.sum(trial_all[...], axis=0)
            trial_gram = wide_gram(trial_wide)
        inverse = inverse_of(trial_gram * time_gram)
        others = proj_all.at[sweep, pl.ds(0, trial_devices - 1)]
        wait_bytes(others, receives[0])

        blocks = [
            proj_all[sweep, k // trials_here, k % trials_here] for k in range(trials)
        ]
        terms = jnp.zeros((comps, neurons_here), jnp.float32)
        for k in range(trials):
            terms = terms + trial_wide[:, comps + k : comps + k + 1] * blocks[k]
        neuron_raw = apply_inverse(inverse, terms)
        payload = split_gram(neuron_raw)
        for k in range(trials):
            total = jnp.sum(neuron_raw * blocks[k], axis=1, keepdims=True)
            payload = jnp.where(lane == comps + k, total, payload)
        half = comps // 2
        folded = payload[:half] + pltpu.roll(payload[half:], LANES // 2, 1)
        gram_all[sweep, 0] = folded

        def start_gram(step):
            pltpu.make_async_remote_copy(
                src_ref=gram_all.at[sweep, 0],
                dst_ref=gram_all.at[sweep, step],
                send_sem=sends[1],
                recv_sem=receives[1],
                device_id=neuron_peer(step),
                device_id_type=MESH,
            ).start()

        each(1, neuron_devices, start_gram)
        wait_bytes(others, sends[0])
        others = gram_all.at[sweep, pl.ds(1, neuron_devices - 1)]
        wait_bytes(others, receives[1])
        folded = jnp.sum(gram_all[sweep], axis=0)
        payload = jnp.concatenate([folded, pltpu.roll(folded, LANES // 2, 1)], axis=0)
        raw_gram = jnp.where(in_gram, payload, 0.0)

        squares = raw_gram * eye
        down = lax.rsqrt(
            jnp.sum(squares, axis=1, keepdims=True) * (1.0 / neurons) + tiny_eps
        )
        across = lax.rsqrt(
            jnp.sum(squares, axis=0, keepdims=True) * (1.0 / neurons) + tiny_eps
        )
        neuron_now = neuron_raw * down
        neuron_gram = raw_gram * down * across
        gram = neuron_gram * time_gram
        scale = 1.0 / mean_trace(gram)
        system = jnp.where(
            in_gram,
            gram * scale + ridge_share * eye,
            jnp.where(in_terms, payload * down * scale, 0.0),
        )
        system = eliminate(system)
        trial_wide = jnp.where(in_terms, system, 0.0)
        own = [
            jnp.sum(
                jnp.where(
                    lane == comps + my_trial * trials_here + k, trial_wide, 0.0
                ),
                axis=1,
                keepdims=True,
            )
            for k in range(trials_here)
        ]

        weights = jnp.concatenate(
            [(neuron_now * own[k]).astype(jnp.bfloat16) for k in range(trials_here)],
            axis=1,
        )
        columns = by_columns and sweep == SWEEPS - 1
        local = jnp.dot(weights, tensor_v[...], preferred_element_type=jnp.float32)
        for c in range(chunks):
            for g in range(groups):
                if columns:
                    tile = None
                    for h in range(groups):
                        part = local[
                            h * ROWS : (h + 1) * ROWS, c * LANES : (c + 1) * LANES
                        ]
                        if h != g:
                            part = pltpu.roll(part, ((h - g) * share) % LANES, 1)
                        tile = part if h == 0 else jnp.where(lane8 < h * share, tile, part)
                else:
                    tile = local[
                        g * ROWS : (g + 1) * ROWS, c * LANES : (c + 1) * LANES
                    ]
                time_local[sweep, c * groups + g] = tile
        my_unit = me // stride

        def start_part(step):
            unit = lax.rem(my_unit + step, units)
            owner = unit * stride
            slot = lax.rem(owner - me + devices, devices)
            pltpu.make_async_remote_copy(
                src_ref=time_local.at[sweep, pl.ds(unit * per, per)],
                dst_ref=time_parts.at[sweep, slot],
                send_sem=sends[2],
                recv_sem=receives[2],
                device_id=device_of(owner),
                device_id_type=MESH,
            ).start()

        def start_direct(slot, device):
            unit = device[0] * trial_devices + device[1]
            pltpu.make_async_remote_copy(
                src_ref=time_local.at[sweep, pl.ds(unit * per, per)],
                dst_ref=time_parts.at[sweep, slot],
                send_sem=sends[2],
                recv_sem=receives[2],
                device_id=device,
                device_id_type=MESH,
            ).start()

        if direct:
            each_other(start_direct)
        else:
            each(1, units, start_part)
        if stride > 1:
            pl.when(lax.rem(me, stride) != 0)(lambda: start_part(0))
        trial_gram = wide_gram(trial_wide)
        inverse = inverse_of(neuron_gram * trial_gram)
        wait_bytes(others, sends[1])

        def reduce_and_send():
            wait_bytes(time_parts.at[sweep, pl.ds(1, devices - 1)], receives[2])
            slice_here = pl.ds(my_unit * per, per)
            total = time_local[sweep, slice_here]
            total = total + jnp.sum(time_parts[sweep, pl.ds(1, devices - 1)], axis=0)
            some = time_sums.at[sweep, pl.ds(0, (units - 1) * per)]
            if columns:
                wait_bytes(some, sends[2])
                return total.reshape(ROWS, LANES)
            time_sums[sweep, slice_here] = total
            mine = time_sums.at[sweep, slice_here]

            def start_sum(slot, device):
                pltpu.make_async_remote_copy(
                    src_ref=mine,
                    dst_ref=mine,
                    send_sem=sends[3],
                    recv_sem=receives[3],
                    device_id=device,
                    device_id_type=MESH,
                ).start()

            each_other(start_sum)
            wait_bytes(some, receives[3])
            wait_bytes(some, sends[2])
            wait_bytes(time_parts.at[sweep, pl.ds(1, devices - 1)], sends[3])

        def send_only():
            wait_bytes(time_sums.at[sweep], receives[3])
            wait_bytes(time_sums.at[sweep], sends[2])

        if columns:
            tile = reduce_and_send()
            mine = jnp.concatenate(
                [tile]
                + [pltpu.roll(tile, LANES - g * share, 1) for g in range(1, groups)],
                axis=0,
            )
            time_raw = apply_inverse(inverse, jnp.where(lane < share, mine, 0.0))
            sums = jnp.sum(time_raw * time_raw, axis=1, keepdims=True)
            norm_all[0] = jnp.sum(sums * eye, axis=0, keepdims=True)

            def start_norm(slot, device):
                pltpu.make_async_remote_copy(
                    src_ref=norm_all.at[0],
                    dst_ref=norm_all.at[slot],
                    send_sem=norm_sem.at[0],
                    recv_sem=norm_sem.at[1],
                    device_id=device,
                    device_id_type=MESH,
                ).start()

            each_other(start_norm)
            neuron_out[...] = neuron_now
            for k in range(trials_here):
                trial_out[k : k + 1, :] = jnp.sum(
                    own[k] * eye[:, :comps], axis=0, keepdims=True
                )
            others = norm_all.at[pl.ds(1, devices - 1)]
            wait_bytes(others, norm_sem.at[1])
            sums = jnp.sum(
                jnp.sum(norm_all[...], axis=0) * eye, axis=1, keepdims=True
            )
            down = lax.rsqrt(sums * (1.0 / timepoints) + tiny_eps)
            time_out[...] = (time_raw * down)[:, :share]
            wait_bytes(others, norm_sem.at[0])
            break
        if stride == 1:
            reduce_and_send()
        else:
            pl.when(lax.rem(me, stride) == 0)(reduce_and_send)
            pl.when(lax.rem(me, stride) != 0)(send_only)
        time_terms = jnp.concatenate(
            [
                time_sums[sweep, pl.ds(c * groups, groups)].reshape(comps, LANES)
                for c in range(chunks)
            ],
            axis=1,
        )
        time_raw = apply_inverse(inverse, time_terms)
        down = lax.rsqrt(
            jnp.sum(time_raw * time_raw, axis=1, keepdims=True) * (1.0 / timepoints)
            + tiny_eps
        )
        time_now = time_raw * down
        time_rounded = time_now.astype(jnp.bfloat16)
        if sweep == SWEEPS - 1:
            for c in range(chunks):
                time_keep[c] = time_now[:, c * LANES : (c + 1) * LANES]
            shares = LANES // share
            chunk = time_keep[me // shares]
            shift = lax.rem(LANES - lax.rem(me, shares) * share, LANES)
            time_out[...] = pltpu.roll(chunk, shift, 1)[:, :share]
            neuron_out[...] = neuron_now
            for k in range(trials_here):
                trial_out[k : k + 1, :] = jnp.sum(
                    own[k] * eye[:, :comps], axis=0, keepdims=True
                )


def keep(neuron_in, time_in, trial_in, neuron_out, time_out, trial_out, sem):
    copies = [
        pltpu.make_async_copy(neuron_in, neuron_out, sem.at[0]),
        pltpu.make_async_copy(time_in, time_out, sem.at[1]),
        pltpu.make_async_copy(trial_in, trial_out, sem.at[2]),
    ]
    for copy in copies:
        copy.start()
    for copy in copies:
        copy.wait()


def per_device(neuron_devices, trial_devices, tensor, time_init, trial_init):
    trials_here, neurons_here, timepoints = tensor.shape
    comps = time_init.shape[0]
    devices = neuron_devices * trial_devices
    tiles = (timepoints // LANES) * (comps // ROWS)
    per = tiles // min(devices, tiles)
    f32 = jnp.float32
    vmem = pl.BlockSpec(memory_space=pltpu.VMEM)
    results = pl.pallas_call(
        functools.partial(kernel, neuron_devices, trial_devices),
        out_shape=(
            jax.ShapeDtypeStruct((comps, neurons_here), f32),
            jax.ShapeDtypeStruct((comps, timepoints // devices), f32),
            jax.ShapeDtypeStruct((trials_here, comps), f32),
        ),
        in_specs=[pl.BlockSpec(memory_space=pl.ANY)] * 3,
        out_specs=(vmem, vmem, vmem),
        scratch_shapes=[
            pltpu.VMEM((trials_here * neurons_here, timepoints), jnp.bfloat16),
            pltpu.VMEM((comps, timepoints), f32),
            pltpu.VMEM((trials_here, comps), f32),
            pltpu.VMEM((trial_devices, comps, LANES), f32),
            pltpu.VMEM((SWEEPS, trial_devices, trials_here, comps, neurons_here), f32),
            pltpu.VMEM((SWEEPS, neuron_devices, comps // 2, LANES), f32),
            pltpu.VMEM((SWEEPS, tiles, ROWS, LANES), f32),
            pltpu.VMEM((SWEEPS, devices, per, ROWS, LANES), f32),
            pltpu.VMEM((SWEEPS, tiles, ROWS, LANES), f32),
            pltpu.VMEM((timepoints // LANES, comps, LANES), f32),
            pltpu.VMEM((devices, 1, LANES), f32),
            pltpu.SemaphoreType.DMA((2 + trials_here,)),
            pltpu.SemaphoreType.DMA((2,)),
            pltpu.SemaphoreType.DMA((2,)),
            pltpu.SemaphoreType.DMA((SWEEPS, 4)),
            pltpu.SemaphoreType.DMA((SWEEPS, 4)),
        ],
        compiler_params=pltpu.CompilerParams(
            collective_id=0,
            has_side_effects=True,
            vmem_limit_bytes=56 * 1024 * 1024,
        ),
    )(tensor, time_init, trial_init.T)
    neuron_now, time_now, trial_now = pl.pallas_call(
        keep,
        out_shape=tuple(jax.ShapeDtypeStruct(r.shape, f32) for r in results),
        in_specs=[pl.BlockSpec(memory_space=pl.ANY)] * 3,
        out_specs=(pl.BlockSpec(memory_space=pl.ANY),) * 3,
        scratch_shapes=[pltpu.SemaphoreType.DMA((3,))],
    )(*results)
    return neuron_now, time_now, trial_now.T


def solution(mesh):
    placed = (P("trial", "neuron", None), P(), P(None, "trial"))
    return jax.shard_map(
        functools.partial(per_device, mesh.shape["neuron"], mesh.shape["trial"]),
        mesh=mesh,
        in_specs=placed,
        out_specs=(P(None, "neuron"), P(None, ("neuron", "trial")), P(None, "trial")),
        check_vma=False,
    )
```

```python
import functools

import jax
import jax.numpy as jnp
from jax import lax
from jax.experimental import pallas as pl
from jax.experimental.pallas import tpu as pltpu
from jax.sharding import PartitionSpec as P

SWEEPS = 2

ridge_share = 0.1
tiny_eps = 1e-06
LANES = 128
ROWS = 8
MESH = pl.DeviceIdType.MESH
EXACT = lax.Precision.HIGHEST
NT = (((1,), (1,)), ((), ()))


def each(low, high, step):
    if high - low <= 40:
        for index in range(low, high):
            step(index)
    else:

        def body(index, carry):
            step(index)
            return carry

        lax.fori_loop(low, high, body, 0)


def wait_bytes(ref, sem):
    pltpu.make_async_copy(ref, ref, sem).wait()


def kernel(
    neuron_devices,
    trial_devices,
    tensor_hbm,
    time_hbm,
    trial_hbm,
    neuron_out,
    time_out,
    trial_out,
    tensor_v,
    time_ref,
    trial_ref,
    trial_all,
    proj_all,
    gram_all,
    time_local,
    time_parts,
    share_local,
    share_parts,
    middle,
    share_sums,
    time_keep,
    norm_all,
    load_sem,
    norm_sem,
    trial_sem,
    send_sem,
    recv_sem,
):
    trials_here, neurons_here, timepoints = tensor_hbm.shape
    comps = time_hbm.shape[0]
    devices = neuron_devices * trial_devices
    trials = trials_here * trial_devices
    neurons = neurons_here * neuron_devices
    chunks = timepoints // LANES
    groups = comps // ROWS
    width = timepoints // trial_devices
    my_neuron = lax.axis_index("neuron")
    my_trial = lax.axis_index("trial")
    me = my_neuron * trial_devices + my_trial

    direct = devices <= 64
    share = timepoints // devices
    by_columns = direct and share * groups == LANES
    neuron_ids = [
        lax.rem(my_neuron + step, neuron_devices)
        for step in range(neuron_devices if direct else 0)
    ]
    trial_ids = [lax.rem(my_trial + step, trial_devices) for step in range(trial_devices)]

    def device_of(linear):
        return (linear // trial_devices, lax.rem(linear, trial_devices))

    def each_other(visit):
        if direct:
            for slot in range(1, devices):
                visit(
                    slot,
                    (
                        neuron_ids[slot // trial_devices],
                        trial_ids[slot % trial_devices],
                    ),
                )
        else:
            each(
                1,
                devices,
                lambda step: visit(step, device_of(lax.rem(me + step, devices))),
            )

    time_load = pltpu.make_async_copy(time_hbm, time_ref, load_sem.at[0])
    time_load.start()
    trial_load = pltpu.make_async_copy(trial_hbm, trial_ref, load_sem.at[1])
    trial_load.start()
    loads = []
    for k in range(trials_here):
        load = pltpu.make_async_copy(
            tensor_hbm.at[k],
            tensor_v.at[pl.ds(k * neurons_here, neurons_here)],
            load_sem.at[2 + k],
        )
        load.start()
        loads.append(load)

    barrier = pltpu.get_barrier_semaphore()

    def greet(slot, device):
        pl.semaphore_signal(barrier, inc=1, device_id=device, device_id_type=MESH)

    each_other(greet)

    lane = lax.broadcasted_iota(jnp.int32, (comps, LANES), 1)
    row = lax.broadcasted_iota(jnp.int32, (comps, LANES), 0)
    eye = (lane == row).astype(jnp.float32)
    right_eye = ((lane >= comps) & (lax.rem(lane, comps) == row)).astype(jnp.float32)
    in_gram = lane < comps
    lane8 = lax.broadcasted_iota(jnp.int32, (ROWS, LANES), 1)
    in_low = (lane >= 2 * comps) & (lane < 3 * comps)
    in_terms = (lane >= comps) & (lane < comps + trials)

    def wide_gram(matrix):
        padded = jnp.concatenate(
            [matrix, jnp.zeros((LANES - comps, matrix.shape[1]), matrix.dtype)], axis=0
        )
        return lax.dot_general(
            matrix, padded, NT, precision=EXACT, preferred_element_type=jnp.float32
        )

    def split(matrix):
        high = matrix.astype(jnp.bfloat16)
        return high, (matrix - high.astype(jnp.float32)).astype(jnp.bfloat16)

    def split_gram(matrix):
        high, low = split(matrix)
        left = jnp.concatenate([high, low, high], axis=1)
        right = jnp.concatenate([high, high, low], axis=1)
        blank = jnp.zeros((LANES - comps, right.shape[1]), jnp.bfloat16)
        return lax.dot_general(
            left,
            jnp.concatenate([right, blank], axis=0),
            NT,
            preferred_element_type=jnp.float32,
        )

    def eliminate(system):
        for k in range(0, comps, 4):
            cols = [
                jnp.broadcast_to(system[:, k + j : k + j + 1], (comps, LANES))
                for j in range(4)
            ]
            for pair in (0, 2):
                top, low = k + pair, k + pair + 1
                col0, col1 = cols[pair], cols[pair + 1]
                a, c = col0[top : top + 1, :], col0[low : low + 1, :]
                b, d = col1[top : top + 1, :], col1[low : low + 1, :]
                inverse = 1.0 / (a * d - b * c)
                a, b, c, d = a * inverse, b * inverse, c * inverse, d * inverse

                def step(matrix):
                    row0, row1 = matrix[top : top + 1, :], matrix[low : low + 1, :]
                    new0 = d * row0 - b * row1
                    new1 = a * row1 - c * row0
                    matrix = matrix - col0 * new0 - col1 * new1
                    return jnp.where(
                        row == top, new0, jnp.where(row == low, new1, matrix)
                    )

                if pair == 0:
                    cols[2], cols[3] = step(cols[2]), step(cols[3])
                system = step(system)
        return system

    def mean_trace(gram):
        return jnp.sum(
            jnp.sum(gram * eye, axis=0, keepdims=True), axis=1, keepdims=True
        ) * (1.0 / comps)

    def inverse_of(gram):
        scale = 1.0 / mean_trace(gram)
        system = eliminate((gram * scale + ridge_share * eye) + right_eye * scale)
        low = system - system.astype(jnp.bfloat16).astype(jnp.float32)
        return jnp.where(in_gram, 0.0, jnp.where(in_low, low, system)).astype(
            jnp.bfloat16
        )

    def apply_inverse(inverse, right_hand):
        width = right_hand.shape[1]
        high, low = split(right_hand)
        padded = jnp.concatenate(
            [jnp.zeros((comps, width), jnp.bfloat16), high, high, low], axis=0
        )
        return lax.dot_general(
            inverse,
            padded,
            (((1,), (0,)), ((), ())),
            preferred_element_type=jnp.float32,
        )

    def send_all(source, target, count, target_of, sends, receives):
        def start(step):
            pltpu.make_async_remote_copy(
                src_ref=source,
                dst_ref=target,
                send_sem=sends,
                recv_sem=receives,
                device_id=target_of(step),
                device_id_type=MESH,
            ).start()

        each(1, count, start)

    def trial_peer(step):
        return (my_neuron, trial_ids[step])

    def neuron_peer(step):
        if direct:
            return (neuron_ids[step], my_trial)
        return (lax.rem(my_neuron + step, neuron_devices), my_trial)

    trial_load.wait()
    placed = jnp.zeros((comps, LANES), jnp.float32)
    for k in range(trials_here):
        column = jnp.sum(
            trial_ref[k : k + 1, :] * eye[:, :comps], axis=1, keepdims=True
        )
        placed = jnp.where(
            lane == comps + my_trial * trials_here + k, column, placed
        )
    trial_all[0] = placed
    time_load.wait()
    time_now = time_ref[...]
    time_rounded = time_now.astype(jnp.bfloat16)

    pl.semaphore_wait(barrier, devices - 1)

    def start_trial(step):
        pltpu.make_async_remote_copy(
            src_ref=trial_all.at[0],
            dst_ref=trial_all.at[step],
            send_sem=trial_sem.at[0],
            recv_sem=trial_sem.at[1],
            device_id=trial_peer(step),
            device_id_type=MESH,
        ).start()

    each(1, trial_devices, start_trial)
    for load in loads:
        load.wait()

    trial_wide = None
    trial_gram = None
    for sweep in range(SWEEPS):
        sends = [send_sem.at[sweep, phase] for phase in range(5)]
        receives = [recv_sem.at[sweep, phase] for phase in range(5)]

        projected = lax.dot_general(
            time_rounded, tensor_v[...], NT, preferred_element_type=jnp.float32
        )
        for k in range(trials_here):
            proj_all[sweep, my_trial, k] = projected[
                :, k * neurons_here : (k + 1) * neurons_here
            ]
        mine = proj_all.at[sweep, my_trial]
        send_all(mine, mine, trial_devices, trial_peer, sends[0], receives[0])
        time_gram = split_gram(time_now)
        if sweep == 0:
            others = trial_all.at[pl.ds(1, trial_devices - 1)]
            wait_bytes(others, trial_sem.at[1])
            wait_bytes(others, trial_sem.at[0])
            trial_wide = jnp.sum(trial_all[...], axis=0)
            trial_gram = wide_gram(trial_wide)
        inverse = inverse_of(trial_gram * time_gram)
        others = proj_all.at[sweep, pl.ds(0, trial_devices - 1)]
        wait_bytes(others, receives[0])

        blocks = [
            proj_all[sweep, k // trials_here, k % trials_here] for k in range(trials)
        ]
        terms = jnp.zeros((comps, neurons_here), jnp.float32)
        for k in range(trials):
            terms = terms + trial_wide[:, comps + k : comps + k + 1] * blocks[k]
        neuron_raw = apply_inverse(inverse, terms)
        payload = split_gram(neuron_raw)
        for k in range(trials):
            total = jnp.sum(neuron_raw * blocks[k], axis=1, keepdims=True)
            payload = jnp.where(lane == comps + k, total, payload)
        half = comps // 2
        folded = payload[:half] + pltpu.roll(payload[half:], LANES // 2, 1)
        gram_all[sweep, 0] = folded

        def start_gram(step):
            pltpu.make_async_remote_copy(
                src_ref=gram_all.at[sweep, 0],
                dst_ref=gram_all.at[sweep, step],
                send_sem=sends[1],
                recv_sem=receives[1],
                device_id=neuron_peer(step),
                device_id_type=MESH,
            ).start()

        each(1, neuron_devices, start_gram)
        wait_bytes(others, sends[0])
        others = gram_all.at[sweep, pl.ds(1, neuron_devices - 1)]
        wait_bytes(others, receives[1])
        folded = jnp.sum(gram_all[sweep], axis=0)
        payload = jnp.concatenate([folded, pltpu.roll(folded, LANES // 2, 1)], axis=0)
        raw_gram = jnp.where(in_gram, payload, 0.0)

        squares = raw_gram * eye
        down = lax.rsqrt(
            jnp.sum(squares, axis=1, keepdims=True) * (1.0 / neurons) + tiny_eps
        )
        across = lax.rsqrt(
            jnp.sum(squares, axis=0, keepdims=True) * (1.0 / neurons) + tiny_eps
        )
        neuron_now = neuron_raw * down
        neuron_gram = raw_gram * down * across
        gram = neuron_gram * time_gram
        scale = 1.0 / mean_trace(gram)
        system = jnp.where(
            in_gram,
            gram * scale + ridge_share * eye,
            jnp.where(in_terms, payload * down * scale, 0.0),
        )
        system = eliminate(system)
        trial_wide = jnp.where(in_terms, system, 0.0)
        own = [
            jnp.sum(
                jnp.where(
                    lane == comps + my_trial * trials_here + k, trial_wide, 0.0
                ),
                axis=1,
                keepdims=True,
            )
            for k in range(trials_here)
        ]

        weights = jnp.concatenate(
            [(neuron_now * own[k]).astype(jnp.bfloat16) for k in range(trials_here)],
            axis=1,
        )
        columns = by_columns and sweep == SWEEPS - 1
        local = jnp.dot(weights, tensor_v[...], preferred_element_type=jnp.float32)
        if columns:
            for c in range(chunks):
                for g in range(groups):
                    tile = None
                    for h in range(groups):
                        part = local[
                            h * ROWS : (h + 1) * ROWS, c * LANES : (c + 1) * LANES
                        ]
                        if h != g:
                            part = pltpu.roll(part, ((h - g) * share) % LANES, 1)
                        tile = part if h == 0 else jnp.where(lane8 < h * share, tile, part)
                    time_local[c * groups + g] = tile

            def start_tile(slot, device):
                pltpu.make_async_remote_copy(
                    src_ref=time_local.at[device[0] * trial_devices + device[1]],
                    dst_ref=time_parts.at[slot],
                    send_sem=sends[2],
                    recv_sem=receives[2],
                    device_id=device,
                    device_id_type=MESH,
                ).start()

            each_other(start_tile)
        else:
            for t in range(trial_devices):
                share_local[sweep, t] = local[:, t * width : (t + 1) * width]

            def start_share(step):
                pltpu.make_async_remote_copy(
                    src_ref=share_local.at[sweep, trial_ids[step]],
                    dst_ref=share_parts.at[sweep, step],
                    send_sem=sends[2],
                    recv_sem=receives[2],
                    device_id=trial_peer(step),
                    device_id_type=MESH,
                ).start()

            each(1, trial_devices, start_share)
        trial_gram = wide_gram(trial_wide)
        inverse = inverse_of(neuron_gram * trial_gram)
        wait_bytes(others, sends[1])

        if columns:
            others = time_parts.at[pl.ds(1, devices - 1)]
            wait_bytes(others, receives[2])
            tile = time_local[me] + jnp.sum(time_parts[1:devices], axis=0)
            mine = jnp.concatenate(
                [tile]
                + [pltpu.roll(tile, LANES - g * share, 1) for g in range(1, groups)],
                axis=0,
            )
            time_raw = apply_inverse(inverse, jnp.where(lane < share, mine, 0.0))
            sums = jnp.sum(time_raw * time_raw, axis=1, keepdims=True)
            norm_all[0] = jnp.sum(sums * eye, axis=0, keepdims=True)

            def start_norm(slot, device):
                pltpu.make_async_remote_copy(
                    src_ref=norm_all.at[0],
                    dst_ref=norm_all.at[slot],
                    send_sem=norm_sem.at[0],
                    recv_sem=norm_sem.at[1],
                    device_id=device,
                    device_id_type=MESH,
                ).start()

            each_other(start_norm)
            neuron_out[...] = neuron_now
            for k in range(trials_here):
                trial_out[k : k + 1, :] = jnp.sum(
                    own[k] * eye[:, :comps], axis=0, keepdims=True
                )
            wait_bytes(others, sends[2])
            others = norm_all.at[pl.ds(1, devices - 1)]
            wait_bytes(others, norm_sem.at[1])
            sums = jnp.sum(
                jnp.sum(norm_all[...], axis=0) * eye, axis=1, keepdims=True
            )
            down = lax.rsqrt(sums * (1.0 / timepoints) + tiny_eps)
            time_out[...] = (time_raw * down)[:, :share]
            wait_bytes(others, norm_sem.at[0])
            break

        others = share_parts.at[sweep, pl.ds(1, trial_devices - 1)]
        wait_bytes(others, receives[2])
        total = share_local[sweep, my_trial]
        for t in range(1, trial_devices):
            total = total + share_parts[sweep, t]
        middle[sweep, 0] = total.astype(jnp.bfloat16)

        def start_middle(step):
            pltpu.make_async_remote_copy(
                src_ref=middle.at[sweep, 0],
                dst_ref=middle.at[sweep, step],
                send_sem=sends[3],
                recv_sem=receives[3],
                device_id=neuron_peer(step),
                device_id_type=MESH,
            ).start()

        each(1, neuron_devices, start_middle)
        wait_bytes(others, sends[2])
        others = middle.at[sweep, pl.ds(1, neuron_devices - 1)]
        wait_bytes(others, receives[3])
        share_sums[sweep, my_trial] = jnp.sum(
            middle[sweep].astype(jnp.float32), axis=0
        )
        mine = share_sums.at[sweep, my_trial]
        send_all(mine, mine, trial_devices, trial_peer, sends[4], receives[4])
        wait_bytes(others, sends[3])
        others = share_sums.at[sweep, pl.ds(0, trial_devices - 1)]
        wait_bytes(others, receives[4])
        time_terms = jnp.concatenate(
            [share_sums[sweep, t] for t in range(trial_devices)], axis=1
        )
        time_raw = apply_inverse(inverse, time_terms)
        wait_bytes(others, sends[4])
        down = lax.rsqrt(
            jnp.sum(time_raw * time_raw, axis=1, keepdims=True) * (1.0 / timepoints)
            + tiny_eps
        )
        time_now = time_raw * down
        time_rounded = time_now.astype(jnp.bfloat16)
        if sweep == SWEEPS - 1:
            for c in range(chunks):
                time_keep[c] = time_now[:, c * LANES : (c + 1) * LANES]
            shares = LANES // share
            chunk = time_keep[me // shares]
            shift = lax.rem(LANES - lax.rem(me, shares) * share, LANES)
            time_out[...] = pltpu.roll(chunk, shift, 1)[:, :share]
            neuron_out[...] = neuron_now
            for k in range(trials_here):
                trial_out[k : k + 1, :] = jnp.sum(
                    own[k] * eye[:, :comps], axis=0, keepdims=True
                )


def keep(neuron_in, time_in, trial_in, neuron_out, time_out, trial_out, sem):
    copies = [
        pltpu.make_async_copy(neuron_in, neuron_out, sem.at[0]),
        pltpu.make_async_copy(time_in, time_out, sem.at[1]),
        pltpu.make_async_copy(trial_in, trial_out, sem.at[2]),
    ]
    for copy in copies:
        copy.start()
    for copy in copies:
        copy.wait()


def per_device(neuron_devices, trial_devices, tensor, time_init, trial_init):
    trials_here, neurons_here, timepoints = tensor.shape
    comps = time_init.shape[0]
    devices = neuron_devices * trial_devices
    tiles = (timepoints // LANES) * (comps // ROWS)
    shares = (SWEEPS, trial_devices, comps, timepoints // trial_devices)
    f32 = jnp.float32
    vmem = pl.BlockSpec(memory_space=pltpu.VMEM)
    results = pl.pallas_call(
        functools.partial(kernel, neuron_devices, trial_devices),
        out_shape=(
            jax.ShapeDtypeStruct((comps, neurons_here), f32),
            jax.ShapeDtypeStruct((comps, timepoints // devices), f32),
            jax.ShapeDtypeStruct((trials_here, comps), f32),
        ),
        in_specs=[pl.BlockSpec(memory_space=pl.ANY)] * 3,
        out_specs=(vmem, vmem, vmem),
        scratch_shapes=[
            pltpu.VMEM((trials_here * neurons_here, timepoints), jnp.bfloat16),
            pltpu.VMEM((comps, timepoints), f32),
            pltpu.VMEM((trials_here, comps), f32),
            pltpu.VMEM((trial_devices, comps, LANES), f32),
            pltpu.VMEM((SWEEPS, trial_devices, trials_here, comps, neurons_here), f32),
            pltpu.VMEM((SWEEPS, neuron_devices, comps // 2, LANES), f32),
            pltpu.VMEM((tiles, ROWS, LANES), f32),
            pltpu.VMEM((devices, ROWS, LANES), f32),
            pltpu.VMEM(shares, f32),
            pltpu.VMEM(shares, f32),
            pltpu.VMEM((SWEEPS, neuron_devices) + shares[2:], jnp.bfloat16),
            pltpu.VMEM(shares, f32),
            pltpu.VMEM((timepoints // LANES, comps, LANES), f32),
            pltpu.VMEM((devices, 1, LANES), f32),
            pltpu.SemaphoreType.DMA((2 + trials_here,)),
            pltpu.SemaphoreType.DMA((2,)),
            pltpu.SemaphoreType.DMA((2,)),
            pltpu.SemaphoreType.DMA((SWEEPS, 5)),
            pltpu.SemaphoreType.DMA((SWEEPS, 5)),
        ],
        compiler_params=pltpu.CompilerParams(
            collective_id=0,
            has_side_effects=True,
            vmem_limit_bytes=56 * 1024 * 1024,
        ),
    )(tensor, time_init, trial_init.T)
    neuron_now, time_now, trial_now = pl.pallas_call(
        keep,
        out_shape=tuple(jax.ShapeDtypeStruct(r.shape, f32) for r in results),
        in_specs=[pl.BlockSpec(memory_space=pl.ANY)] * 3,
        out_specs=(pl.BlockSpec(memory_space=pl.ANY),) * 3,
        scratch_shapes=[pltpu.SemaphoreType.DMA((3,))],
    )(*results)
    return neuron_now, time_now, trial_now.T


def solution(mesh):
    placed = (P("trial", "neuron", None), P(), P(None, "trial"))
    return jax.shard_map(
        functools.partial(per_device, mesh.shape["neuron"], mesh.shape["trial"]),
        mesh=mesh,
        in_specs=placed,
        out_specs=(P(None, "neuron"), P(None, ("neuron", "trial")), P(None, "trial")),
        check_vma=False,
    )
```

```python
import functools

import jax
import jax.numpy as jnp
from jax import lax
from jax.experimental import pallas as pl
from jax.experimental.pallas import tpu as pltpu
from jax.sharding import PartitionSpec as P

SWEEPS = 2

ridge_share = 0.1
tiny_eps = 1e-06
LANES = 128
ROWS = 8
MESH = pl.DeviceIdType.MESH
EXACT = lax.Precision.HIGHEST
NT = (((1,), (1,)), ((), ()))


def each(low, high, step):
    if high - low <= 40:
        for index in range(low, high):
            step(index)
    else:

        def body(index, carry):
            step(index)
            return carry

        lax.fori_loop(low, high, body, 0)


def wait_bytes(ref, sem):
    pltpu.make_async_copy(ref, ref, sem).wait()


def kernel(
    neuron_devices,
    trial_devices,
    tensor_hbm,
    time_hbm,
    trial_hbm,
    neuron_out,
    time_out,
    trial_out,
    tensor_v,
    time_ref,
    trial_ref,
    trial_all,
    proj_all,
    gram_all,
    time_local,
    time_parts,
    share_local,
    share_parts,
    middle,
    share_sums,
    time_keep,
    norm_all,
    load_sem,
    norm_sem,
    trial_sem,
    send_sem,
    recv_sem,
):
    trials_here, neurons_here, timepoints = tensor_hbm.shape
    comps = time_hbm.shape[0]
    devices = neuron_devices * trial_devices
    trials = trials_here * trial_devices
    neurons = neurons_here * neuron_devices
    chunks = timepoints // LANES
    groups = comps // ROWS
    width = timepoints // trial_devices
    my_neuron = lax.axis_index("neuron")
    my_trial = lax.axis_index("trial")
    me = my_neuron * trial_devices + my_trial

    direct = devices <= 64
    share = timepoints // devices
    by_columns = direct and share * groups == LANES
    neuron_ids = [
        lax.rem(my_neuron + step, neuron_devices)
        for step in range(neuron_devices if direct else 0)
    ]
    trial_ids = [lax.rem(my_trial + step, trial_devices) for step in range(trial_devices)]

    def device_of(linear):
        return (linear // trial_devices, lax.rem(linear, trial_devices))

    def each_other(visit):
        if direct:
            for slot in range(1, devices):
                visit(
                    slot,
                    (
                        neuron_ids[slot // trial_devices],
                        trial_ids[slot % trial_devices],
                    ),
                )
        else:
            each(
                1,
                devices,
                lambda step: visit(step, device_of(lax.rem(me + step, devices))),
            )

    time_load = pltpu.make_async_copy(time_hbm, time_ref, load_sem.at[0])
    time_load.start()
    trial_load = pltpu.make_async_copy(trial_hbm, trial_ref, load_sem.at[1])
    trial_load.start()
    loads = []
    for k in range(trials_here):
        load = pltpu.make_async_copy(
            tensor_hbm.at[k],
            tensor_v.at[pl.ds(k * neurons_here, neurons_here)],
            load_sem.at[2 + k],
        )
        load.start()
        loads.append(load)

    barrier = pltpu.get_barrier_semaphore()

    def greet(slot, device):
        pl.semaphore_signal(barrier, inc=1, device_id=device, device_id_type=MESH)

    each_other(greet)

    lane = lax.broadcasted_iota(jnp.int32, (comps, LANES), 1)
    row = lax.broadcasted_iota(jnp.int32, (comps, LANES), 0)
    eye = (lane == row).astype(jnp.float32)
    right_eye = ((lane >= comps) & (lax.rem(lane, comps) == row)).astype(jnp.float32)
    in_gram = lane < comps
    lane8 = lax.broadcasted_iota(jnp.int32, (ROWS, LANES), 1)
    in_low = (lane >= 2 * comps) & (lane < 3 * comps)
    in_terms = (lane >= comps) & (lane < comps + trials)

    def wide_gram(matrix):
        padded = jnp.concatenate(
            [matrix, jnp.zeros((LANES - comps, matrix.shape[1]), matrix.dtype)], axis=0
        )
        return lax.dot_general(
            matrix, padded, NT, precision=EXACT, preferred_element_type=jnp.float32
        )

    def split(matrix):
        high = matrix.astype(jnp.bfloat16)
        return high, (matrix - high.astype(jnp.float32)).astype(jnp.bfloat16)

    def split_gram(matrix):
        high, low = split(matrix)
        left = jnp.concatenate([high, low, high], axis=1)
        right = jnp.concatenate([high, high, low], axis=1)
        blank = jnp.zeros((LANES - comps, right.shape[1]), jnp.bfloat16)
        return lax.dot_general(
            left,
            jnp.concatenate([right, blank], axis=0),
            NT,
            preferred_element_type=jnp.float32,
        )

    def eliminate(system):
        spread = (ROWS, LANES)
        parts = [system[v * ROWS : (v + 1) * ROWS] for v in range(groups)]
        row8 = lax.broadcasted_iota(jnp.int32, spread, 0)
        for k in range(0, comps, 4):
            home, at = k // ROWS, k % ROWS
            cols = [
                [jnp.broadcast_to(part[:, k + j : k + j + 1], spread) for part in parts]
                for j in range(4)
            ]
            rows = [
                jnp.broadcast_to(parts[home][at + j : at + j + 1, :], spread)
                for j in range(4)
            ]
            e = {}
            for x in range(4):
                for y in range(x, 4):
                    e[x, y] = jnp.broadcast_to(
                        cols[y][home][at + x : at + x + 1, :], spread
                    )
            inverse = 1.0 / (e[0, 0] * e[1, 1] - e[0, 1] * e[0, 1])
            a, b, d = e[1, 1] * inverse, -e[0, 1] * inverse, e[0, 0] * inverse
            t02 = a * e[0, 2] + b * e[1, 2]
            t03 = a * e[0, 3] + b * e[1, 3]
            t12 = b * e[0, 2] + d * e[1, 2]
            t13 = b * e[0, 3] + d * e[1, 3]
            s22 = e[2, 2] - (e[0, 2] * t02 + e[1, 2] * t12)
            s23 = e[2, 3] - (e[0, 2] * t03 + e[1, 2] * t13)
            s33 = e[3, 3] - (e[0, 3] * t03 + e[1, 3] * t13)
            inverse = 1.0 / (s22 * s33 - s23 * s23)
            low2 = rows[2] - (t02 * rows[0] + t12 * rows[1])
            low3 = rows[3] - (t03 * rows[0] + t13 * rows[1])
            new2 = (s33 * low2 - s23 * low3) * inverse
            new3 = (s22 * low3 - s23 * low2) * inverse
            new0 = (a * rows[0] + b * rows[1]) - (t02 * new2 + t03 * new3)
            new1 = (b * rows[0] + d * rows[1]) - (t12 * new2 + t13 * new3)
            news = [new0, new1, new2, new3]
            parts = [
                parts[v]
                - (cols[2][v] * new2 + cols[3][v] * new3)
                - (cols[0][v] * new0 + cols[1][v] * new1)
                for v in range(groups)
            ]
            for j in range(4):
                parts[home] = jnp.where(row8 == at + j, news[j], parts[home])
        return jnp.concatenate(parts, axis=0)

    def mean_trace(gram):
        return jnp.sum(
            jnp.sum(gram * eye, axis=0, keepdims=True), axis=1, keepdims=True
        ) * (1.0 / comps)

    def inverse_of(gram):
        scale = 1.0 / mean_trace(gram)
        system = eliminate((gram * scale + ridge_share * eye) + right_eye * scale)
        low = system - system.astype(jnp.bfloat16).astype(jnp.float32)
        return jnp.where(in_gram, 0.0, jnp.where(in_low, low, system)).astype(
            jnp.bfloat16
        )

    def apply_inverse(inverse, right_hand):
        width = right_hand.shape[1]
        high, low = split(right_hand)
        padded = jnp.concatenate(
            [jnp.zeros((comps, width), jnp.bfloat16), high, high, low], axis=0
        )
        return lax.dot_general(
            inverse,
            padded,
            (((1,), (0,)), ((), ())),
            preferred_element_type=jnp.float32,
        )

    def send_all(source, target, count, target_of, sends, receives):
        def start(step):
            pltpu.make_async_remote_copy(
                src_ref=source,
                dst_ref=target,
                send_sem=sends,
                recv_sem=receives,
                device_id=target_of(step),
                device_id_type=MESH,
            ).start()

        each(1, count, start)

    def trial_peer(step):
        return (my_neuron, trial_ids[step])

    def neuron_peer(step):
        if direct:
            return (neuron_ids[step], my_trial)
        return (lax.rem(my_neuron + step, neuron_devices), my_trial)

    trial_load.wait()
    placed = jnp.zeros((comps, LANES), jnp.float32)
    for k in range(trials_here):
        column = jnp.sum(
            trial_ref[k : k + 1, :] * eye[:, :comps], axis=1, keepdims=True
        )
        placed = jnp.where(
            lane == comps + my_trial * trials_here + k, column, placed
        )
    trial_all[0] = placed
    time_load.wait()
    time_now = time_ref[...]
    time_rounded = time_now.astype(jnp.bfloat16)

    pl.semaphore_wait(barrier, devices - 1)

    def start_trial(step):
        pltpu.make_async_remote_copy(
            src_ref=trial_all.at[0],
            dst_ref=trial_all.at[step],
            send_sem=trial_sem.at[0],
            recv_sem=trial_sem.at[1],
            device_id=trial_peer(step),
            device_id_type=MESH,
        ).start()

    each(1, trial_devices, start_trial)
    for load in loads:
        load.wait()

    trial_wide = None
    trial_gram = None
    for sweep in range(SWEEPS):
        sends = [send_sem.at[sweep, phase] for phase in range(5)]
        receives = [recv_sem.at[sweep, phase] for phase in range(5)]

        projected = lax.dot_general(
            time_rounded, tensor_v[...], NT, preferred_element_type=jnp.float32
        )
        for k in range(trials_here):
            proj_all[sweep, my_trial, k] = projected[
                :, k * neurons_here : (k + 1) * neurons_here
            ].astype(jnp.bfloat16)
        mine = proj_all.at[sweep, my_trial]
        send_all(mine, mine, trial_devices, trial_peer, sends[0], receives[0])
        time_gram = split_gram(time_now)
        if sweep == 0:
            others = trial_all.at[pl.ds(1, trial_devices - 1)]
            wait_bytes(others, trial_sem.at[1])
            wait_bytes(others, trial_sem.at[0])
            trial_wide = jnp.sum(trial_all[...], axis=0)
            trial_gram = wide_gram(trial_wide)
        inverse = inverse_of(trial_gram * time_gram)
        others = proj_all.at[sweep, pl.ds(0, trial_devices - 1)]
        wait_bytes(others, receives[0])

        blocks = [
            proj_all[sweep, k // trials_here, k % trials_here].astype(jnp.float32)
            for k in range(trials)
        ]
        terms = jnp.zeros((comps, neurons_here), jnp.float32)
        for k in range(trials):
            terms = terms + trial_wide[:, comps + k : comps + k + 1] * blocks[k]
        neuron_raw = apply_inverse(inverse, terms)
        payload = split_gram(neuron_raw)
        for k in range(trials):
            total = jnp.sum(neuron_raw * blocks[k], axis=1, keepdims=True)
            payload = jnp.where(lane == comps + k, total, payload)
        half = comps // 2
        folded = payload[:half] + pltpu.roll(payload[half:], LANES // 2, 1)
        gram_all[sweep, 0] = folded

        def start_gram(step):
            pltpu.make_async_remote_copy(
                src_ref=gram_all.at[sweep, 0],
                dst_ref=gram_all.at[sweep, step],
                send_sem=sends[1],
                recv_sem=receives[1],
                device_id=neuron_peer(step),
                device_id_type=MESH,
            ).start()

        each(1, neuron_devices, start_gram)
        wait_bytes(others, sends[0])
        others = gram_all.at[sweep, pl.ds(1, neuron_devices - 1)]
        wait_bytes(others, receives[1])
        folded = jnp.sum(gram_all[sweep], axis=0)
        payload = jnp.concatenate([folded, pltpu.roll(folded, LANES // 2, 1)], axis=0)
        raw_gram = jnp.where(in_gram, payload, 0.0)

        squares = raw_gram * eye
        down = lax.rsqrt(
            jnp.sum(squares, axis=1, keepdims=True) * (1.0 / neurons) + tiny_eps
        )
        across = lax.rsqrt(
            jnp.sum(squares, axis=0, keepdims=True) * (1.0 / neurons) + tiny_eps
        )
        neuron_now = neuron_raw * down
        neuron_gram = raw_gram * down * across
        gram = neuron_gram * time_gram
        scale = 1.0 / mean_trace(gram)
        system = jnp.where(
            in_gram,
            gram * scale + ridge_share * eye,
            jnp.where(in_terms, payload * down * scale, 0.0),
        )
        system = eliminate(system)
        trial_wide = jnp.where(in_terms, system, 0.0)
        own = [
            jnp.sum(
                jnp.where(
                    lane == comps + my_trial * trials_here + k, trial_wide, 0.0
                ),
                axis=1,
                keepdims=True,
            )
            for k in range(trials_here)
        ]

        weights = jnp.concatenate(
            [(neuron_now * own[k]).astype(jnp.bfloat16) for k in range(trials_here)],
            axis=1,
        )
        columns = by_columns and sweep == SWEEPS - 1
        local = jnp.dot(weights, tensor_v[...], preferred_element_type=jnp.float32)
        if columns:
            for c in range(chunks):
                for g in range(groups):
                    tile = None
                    for h in range(groups):
                        part = local[
                            h * ROWS : (h + 1) * ROWS, c * LANES : (c + 1) * LANES
                        ]
                        if h != g:
                            part = pltpu.roll(part, ((h - g) * share) % LANES, 1)
                        tile = part if h == 0 else jnp.where(lane8 < h * share, tile, part)
                    time_local[c * groups + g] = tile

            def start_tile(slot, device):
                pltpu.make_async_remote_copy(
                    src_ref=time_local.at[device[0] * trial_devices + device[1]],
                    dst_ref=time_parts.at[slot],
                    send_sem=sends[2],
                    recv_sem=receives[2],
                    device_id=device,
                    device_id_type=MESH,
                ).start()

            each_other(start_tile)
        else:
            for t in range(trial_devices):
                share_local[sweep, t] = local[:, t * width : (t + 1) * width]

            def start_share(step):
                pltpu.make_async_remote_copy(
                    src_ref=share_local.at[sweep, trial_ids[step]],
                    dst_ref=share_parts.at[sweep, step],
                    send_sem=sends[2],
                    recv_sem=receives[2],
                    device_id=trial_peer(step),
                    device_id_type=MESH,
                ).start()

            each(1, trial_devices, start_share)
        trial_gram = wide_gram(trial_wide)
        inverse = inverse_of(neuron_gram * trial_gram)
        wait_bytes(others, sends[1])

        if columns:
            others = time_parts.at[pl.ds(1, devices - 1)]
            wait_bytes(others, receives[2])
            tile = time_local[me] + jnp.sum(time_parts[1:devices], axis=0)
            mine = jnp.concatenate(
                [tile]
                + [pltpu.roll(tile, LANES - g * share, 1) for g in range(1, groups)],
                axis=0,
            )
            time_raw = apply_inverse(inverse, jnp.where(lane < share, mine, 0.0))
            sums = jnp.sum(time_raw * time_raw, axis=1, keepdims=True)
            norm_all[0] = jnp.sum(sums * eye, axis=0, keepdims=True)

            def start_norm(slot, device):
                pltpu.make_async_remote_copy(
                    src_ref=norm_all.at[0],
                    dst_ref=norm_all.at[slot],
                    send_sem=norm_sem.at[0],
                    recv_sem=norm_sem.at[1],
                    device_id=device,
                    device_id_type=MESH,
                ).start()

            each_other(start_norm)
            neuron_out[...] = neuron_now
            for k in range(trials_here):
                trial_out[k : k + 1, :] = jnp.sum(
                    own[k] * eye[:, :comps], axis=0, keepdims=True
                )
            wait_bytes(others, sends[2])
            others = norm_all.at[pl.ds(1, devices - 1)]
            wait_bytes(others, norm_sem.at[1])
            sums = jnp.sum(
                jnp.sum(norm_all[...], axis=0) * eye, axis=1, keepdims=True
            )
            down = lax.rsqrt(sums * (1.0 / timepoints) + tiny_eps)
            time_out[...] = (time_raw * down)[:, :share]
            wait_bytes(others, norm_sem.at[0])
            break

        others = share_parts.at[sweep, pl.ds(1, trial_devices - 1)]
        wait_bytes(others, receives[2])
        total = share_local[sweep, my_trial]
        for t in range(1, trial_devices):
            total = total + share_parts[sweep, t]
        middle[sweep, 0] = total.astype(jnp.bfloat16)

        def start_middle(step):
            pltpu.make_async_remote_copy(
                src_ref=middle.at[sweep, 0],
                dst_ref=middle.at[sweep, step],
                send_sem=sends[3],
                recv_sem=receives[3],
                device_id=neuron_peer(step),
                device_id_type=MESH,
            ).start()

        each(1, neuron_devices, start_middle)
        wait_bytes(others, sends[2])
        others = middle.at[sweep, pl.ds(1, neuron_devices - 1)]
        wait_bytes(others, receives[3])
        share_sums[sweep, my_trial] = jnp.sum(
            middle[sweep].astype(jnp.float32), axis=0
        )
        mine = share_sums.at[sweep, my_trial]
        send_all(mine, mine, trial_devices, trial_peer, sends[4], receives[4])
        wait_bytes(others, sends[3])
        others = share_sums.at[sweep, pl.ds(0, trial_devices - 1)]
        wait_bytes(others, receives[4])
        time_terms = jnp.concatenate(
            [share_sums[sweep, t] for t in range(trial_devices)], axis=1
        )
        time_raw = apply_inverse(inverse, time_terms)
        wait_bytes(others, sends[4])
        down = lax.rsqrt(
            jnp.sum(time_raw * time_raw, axis=1, keepdims=True) * (1.0 / timepoints)
            + tiny_eps
        )
        time_now = time_raw * down
        time_rounded = time_now.astype(jnp.bfloat16)
        if sweep == SWEEPS - 1:
            for c in range(chunks):
                time_keep[c] = time_now[:, c * LANES : (c + 1) * LANES]
            shares = LANES // share
            chunk = time_keep[me // shares]
            shift = lax.rem(LANES - lax.rem(me, shares) * share, LANES)
            time_out[...] = pltpu.roll(chunk, shift, 1)[:, :share]
            neuron_out[...] = neuron_now
            for k in range(trials_here):
                trial_out[k : k + 1, :] = jnp.sum(
                    own[k] * eye[:, :comps], axis=0, keepdims=True
                )


def keep(neuron_in, time_in, trial_in, neuron_out, time_out, trial_out, sem):
    copies = [
        pltpu.make_async_copy(neuron_in, neuron_out, sem.at[0]),
        pltpu.make_async_copy(time_in, time_out, sem.at[1]),
        pltpu.make_async_copy(trial_in, trial_out, sem.at[2]),
    ]
    for copy in copies:
        copy.start()
    for copy in copies:
        copy.wait()


def per_device(neuron_devices, trial_devices, tensor, time_init, trial_init):
    trials_here, neurons_here, timepoints = tensor.shape
    comps = time_init.shape[0]
    devices = neuron_devices * trial_devices
    tiles = (timepoints // LANES) * (comps // ROWS)
    shares = (SWEEPS, trial_devices, comps, timepoints // trial_devices)
    f32 = jnp.float32
    vmem = pl.BlockSpec(memory_space=pltpu.VMEM)
    results = pl.pallas_call(
        functools.partial(kernel, neuron_devices, trial_devices),
        out_shape=(
            jax.ShapeDtypeStruct((comps, neurons_here), f32),
            jax.ShapeDtypeStruct((comps, timepoints // devices), f32),
            jax.ShapeDtypeStruct((trials_here, comps), f32),
        ),
        in_specs=[pl.BlockSpec(memory_space=pl.ANY)] * 3,
        out_specs=(vmem, vmem, vmem),
        scratch_shapes=[
            pltpu.VMEM((trials_here * neurons_here, timepoints), jnp.bfloat16),
            pltpu.VMEM((comps, timepoints), f32),
            pltpu.VMEM((trials_here, comps), f32),
            pltpu.VMEM((trial_devices, comps, LANES), f32),
            pltpu.VMEM(
                (SWEEPS, trial_devices, trials_here, comps, neurons_here), jnp.bfloat16
            ),
            pltpu.VMEM((SWEEPS, neuron_devices, comps // 2, LANES), f32),
            pltpu.VMEM((tiles, ROWS, LANES), f32),
            pltpu.VMEM((devices, ROWS, LANES), f32),
            pltpu.VMEM(shares, f32),
            pltpu.VMEM(shares, f32),
            pltpu.VMEM((SWEEPS, neuron_devices) + shares[2:], jnp.bfloat16),
            pltpu.VMEM(shares, f32),
            pltpu.VMEM((timepoints // LANES, comps, LANES), f32),
            pltpu.VMEM((devices, 1, LANES), f32),
            pltpu.SemaphoreType.DMA((2 + trials_here,)),
            pltpu.SemaphoreType.DMA((2,)),
            pltpu.SemaphoreType.DMA((2,)),
            pltpu.SemaphoreType.DMA((SWEEPS, 5)),
            pltpu.SemaphoreType.DMA((SWEEPS, 5)),
        ],
        compiler_params=pltpu.CompilerParams(
            collective_id=0,
            has_side_effects=True,
            vmem_limit_bytes=56 * 1024 * 1024,
        ),
    )(tensor, time_init, trial_init.T)
    neuron_now, time_now, trial_now = pl.pallas_call(
        keep,
        out_shape=tuple(jax.ShapeDtypeStruct(r.shape, f32) for r in results),
        in_specs=[pl.BlockSpec(memory_space=pl.ANY)] * 3,
        out_specs=(pl.BlockSpec(memory_space=pl.ANY),) * 3,
        scratch_shapes=[pltpu.SemaphoreType.DMA((3,))],
    )(*results)
    return neuron_now, time_now, trial_now.T


def solution(mesh):
    placed = (P("trial", "neuron", None), P(), P(None, "trial"))
    return jax.shard_map(
        functools.partial(per_device, mesh.shape["neuron"], mesh.shape["trial"]),
        mesh=mesh,
        in_specs=placed,
        out_specs=(P(None, "neuron"), P(None, ("neuron", "trial")), P(None, "trial")),
        check_vma=False,
    )
```

```python
import functools

import jax
import jax.numpy as jnp
from jax import lax
from jax.experimental import pallas as pl
from jax.experimental.pallas import tpu as pltpu
from jax.sharding import PartitionSpec as P

SWEEPS = 2

ridge_share = 0.1
tiny_eps = 1e-06
LANES = 128
ROWS = 8
MESH = pl.DeviceIdType.MESH
NT = (((1,), (1,)), ((), ()))


def each(low, high, step):
    if high - low <= 40:
        for index in range(low, high):
            step(index)
    else:

        def body(index, carry):
            step(index)
            return carry

        lax.fori_loop(low, high, body, 0)


def wait_bytes(ref, sem):
    pltpu.make_async_copy(ref, ref, sem).wait()


def kernel(
    neuron_devices,
    trial_devices,
    tensor_hbm,
    time_hbm,
    trial_hbm,
    neuron_out,
    time_out,
    trial_out,
    tensor_v,
    time_ref,
    trial_ref,
    trial_all,
    proj_all,
    gram_all,
    time_local,
    time_parts,
    share_local,
    share_parts,
    middle,
    share_sums,
    time_keep,
    norm_all,
    load_sem,
    norm_sem,
    trial_sem,
    send_sem,
    recv_sem,
):
    trials_here, neurons_here, timepoints = tensor_hbm.shape
    comps = time_hbm.shape[0]
    devices = neuron_devices * trial_devices
    trials = trials_here * trial_devices
    neurons = neurons_here * neuron_devices
    chunks = timepoints // LANES
    groups = comps // ROWS
    width = timepoints // trial_devices
    my_neuron = lax.axis_index("neuron")
    my_trial = lax.axis_index("trial")
    me = my_neuron * trial_devices + my_trial

    direct = devices <= 64
    share = timepoints // devices
    by_columns = direct and share * groups == LANES
    neuron_ids = [
        lax.rem(my_neuron + step, neuron_devices)
        for step in range(neuron_devices if direct else 0)
    ]
    trial_ids = [lax.rem(my_trial + step, trial_devices) for step in range(trial_devices)]

    def device_of(linear):
        return (linear // trial_devices, lax.rem(linear, trial_devices))

    def each_other(visit):
        if direct:
            for slot in range(1, devices):
                visit(
                    slot,
                    (
                        neuron_ids[slot // trial_devices],
                        trial_ids[slot % trial_devices],
                    ),
                )
        else:
            each(
                1,
                devices,
                lambda step: visit(step, device_of(lax.rem(me + step, devices))),
            )

    time_load = pltpu.make_async_copy(time_hbm, time_ref, load_sem.at[0])
    time_load.start()
    trial_load = pltpu.make_async_copy(trial_hbm, trial_ref, load_sem.at[1])
    trial_load.start()
    loads = []
    for k in range(trials_here):
        load = pltpu.make_async_copy(
            tensor_hbm.at[k],
            tensor_v.at[pl.ds(k * neurons_here, neurons_here)],
            load_sem.at[2 + k],
        )
        load.start()
        loads.append(load)

    barrier = pltpu.get_barrier_semaphore()

    def greet(slot, device):
        pl.semaphore_signal(barrier, inc=1, device_id=device, device_id_type=MESH)

    each_other(greet)

    lane = lax.broadcasted_iota(jnp.int32, (comps, LANES), 1)
    row = lax.broadcasted_iota(jnp.int32, (comps, LANES), 0)
    eye = (lane == row).astype(jnp.float32)
    right_eye = ((lane >= comps) & (lax.rem(lane, comps) == row)).astype(jnp.float32)
    in_gram = lane < comps
    lane8 = lax.broadcasted_iota(jnp.int32, (ROWS, LANES), 1)
    in_low = (lane >= 2 * comps) & (lane < 3 * comps)
    in_terms = (lane >= comps) & (lane < comps + trials)

    def widen(gram):
        blank = jnp.zeros((comps, LANES - comps), jnp.float32)
        return jnp.concatenate([gram, blank], axis=1)

    def split(matrix):
        high = matrix.astype(jnp.bfloat16)
        return high, (matrix - high.astype(jnp.float32)).astype(jnp.bfloat16)

    def split_gram(matrix):
        high, low = split(matrix)
        left = jnp.concatenate([high, low, high], axis=1)
        right = jnp.concatenate([high, high, low], axis=1)
        gram = lax.dot_general(left, right, NT, preferred_element_type=jnp.float32)
        return widen(gram)

    def eliminate(system):
        for k in range(0, comps, 4):
            cols = [
                jnp.broadcast_to(system[:, k + j : k + j + 1], (comps, LANES))
                for j in range(4)
            ]
            for pair in (0, 2):
                top, low = k + pair, k + pair + 1
                col0, col1 = cols[pair], cols[pair + 1]
                a, c = col0[top : top + 1, :], col0[low : low + 1, :]
                b, d = col1[top : top + 1, :], col1[low : low + 1, :]
                inverse = 1.0 / (a * d - b * c)
                a, b, c, d = a * inverse, b * inverse, c * inverse, d * inverse

                def step(matrix):
                    row0, row1 = matrix[top : top + 1, :], matrix[low : low + 1, :]
                    new0 = d * row0 - b * row1
                    new1 = a * row1 - c * row0
                    matrix = matrix - col0 * new0 - col1 * new1
                    return jnp.where(
                        row == top, new0, jnp.where(row == low, new1, matrix)
                    )

                if pair == 0:
                    cols[2], cols[3] = step(cols[2]), step(cols[3])
                system = step(system)
        return system

    def mean_trace(gram):
        return jnp.sum(
            jnp.sum(gram * eye, axis=0, keepdims=True), axis=1, keepdims=True
        ) * (1.0 / comps)

    def inverse_of(gram):
        scale = 1.0 / mean_trace(gram)
        system = eliminate((gram * scale + ridge_share * eye) + right_eye * scale)
        low = system - system.astype(jnp.bfloat16).astype(jnp.float32)
        return jnp.where(in_gram, 0.0, jnp.where(in_low, low, system)).astype(
            jnp.bfloat16
        )

    def apply_inverse(inverse, right_hand):
        width = right_hand.shape[1]
        high, low = split(right_hand)
        padded = jnp.concatenate(
            [jnp.zeros((comps, width), jnp.bfloat16), high, high, low], axis=0
        )
        return lax.dot_general(
            inverse,
            padded,
            (((1,), (0,)), ((), ())),
            preferred_element_type=jnp.float32,
        )

    def send_all(source, target, count, target_of, sends, receives):
        def start(step):
            pltpu.make_async_remote_copy(
                src_ref=source,
                dst_ref=target,
                send_sem=sends,
                recv_sem=receives,
                device_id=target_of(step),
                device_id_type=MESH,
            ).start()

        each(1, count, start)

    def trial_peer(step):
        return (my_neuron, trial_ids[step])

    def neuron_peer(step):
        if direct:
            return (neuron_ids[step], my_trial)
        return (lax.rem(my_neuron + step, neuron_devices), my_trial)

    trial_load.wait()
    placed = jnp.zeros((comps, LANES), jnp.float32)
    for k in range(trials_here):
        column = jnp.sum(
            trial_ref[k : k + 1, :] * eye[:, :comps], axis=1, keepdims=True
        )
        placed = jnp.where(
            lane == comps + my_trial * trials_here + k, column, placed
        )
    trial_all[0] = placed
    time_load.wait()
    time_now = time_ref[...]
    time_rounded = time_now.astype(jnp.bfloat16)

    pl.semaphore_wait(barrier, devices - 1)

    def start_trial(step):
        pltpu.make_async_remote_copy(
            src_ref=trial_all.at[0],
            dst_ref=trial_all.at[step],
            send_sem=trial_sem.at[0],
            recv_sem=trial_sem.at[1],
            device_id=trial_peer(step),
            device_id_type=MESH,
        ).start()

    each(1, trial_devices, start_trial)
    for load in loads:
        load.wait()

    trial_wide = None
    trial_gram = None
    for sweep in range(SWEEPS):
        sends = [send_sem.at[sweep, phase] for phase in range(5)]
        receives = [recv_sem.at[sweep, phase] for phase in range(5)]

        projected = lax.dot_general(
            time_rounded, tensor_v[...], NT, preferred_element_type=jnp.float32
        )
        for k in range(trials_here):
            proj_all[sweep, my_trial, k] = projected[
                :, k * neurons_here : (k + 1) * neurons_here
            ]
        mine = proj_all.at[sweep, my_trial]
        send_all(mine, mine, trial_devices, trial_peer, sends[0], receives[0])
        time_gram = split_gram(time_now)
        if sweep == 0:
            others = trial_all.at[pl.ds(1, trial_devices - 1)]
            wait_bytes(others, trial_sem.at[1])
            wait_bytes(others, trial_sem.at[0])
            trial_wide = jnp.sum(trial_all[...], axis=0)
            trial_gram = split_gram(trial_wide)
        inverse = inverse_of(trial_gram * time_gram)
        others = proj_all.at[sweep, pl.ds(0, trial_devices - 1)]
        wait_bytes(others, receives[0])

        blocks = [
            proj_all[sweep, k // trials_here, k % trials_here] for k in range(trials)
        ]
        terms = jnp.zeros((comps, neurons_here), jnp.float32)
        for k in range(trials):
            terms = terms + trial_wide[:, comps + k : comps + k + 1] * blocks[k]
        neuron_raw = apply_inverse(inverse, terms)
        payload = split_gram(neuron_raw)
        for k in range(trials):
            total = jnp.sum(neuron_raw * blocks[k], axis=1, keepdims=True)
            payload = jnp.where(lane == comps + k, total, payload)
        half = comps // 2
        folded = payload[:half] + pltpu.roll(payload[half:], LANES // 2, 1)
        gram_all[sweep, 0] = folded

        def start_gram(step):
            pltpu.make_async_remote_copy(
                src_ref=gram_all.at[sweep, 0],
                dst_ref=gram_all.at[sweep, step],
                send_sem=sends[1],
                recv_sem=receives[1],
                device_id=neuron_peer(step),
                device_id_type=MESH,
            ).start()

        each(1, neuron_devices, start_gram)
        wait_bytes(others, sends[0])
        others = gram_all.at[sweep, pl.ds(1, neuron_devices - 1)]
        wait_bytes(others, receives[1])
        folded = jnp.sum(gram_all[sweep], axis=0)
        payload = jnp.concatenate([folded, pltpu.roll(folded, LANES // 2, 1)], axis=0)
        raw_gram = jnp.where(in_gram, payload, 0.0)

        squares = raw_gram * eye
        down = lax.rsqrt(
            jnp.sum(squares, axis=1, keepdims=True) * (1.0 / neurons) + tiny_eps
        )
        across = lax.rsqrt(
            jnp.sum(squares, axis=0, keepdims=True) * (1.0 / neurons) + tiny_eps
        )
        neuron_now = neuron_raw * down
        neuron_gram = raw_gram * down * across
        gram = neuron_gram * time_gram
        scale = 1.0 / mean_trace(gram)
        system = jnp.where(
            in_gram,
            gram * scale + ridge_share * eye,
            jnp.where(in_terms, payload * down * scale, 0.0),
        )
        system = eliminate(system)
        trial_wide = jnp.where(in_terms, system, 0.0)
        own = [
            jnp.sum(
                jnp.where(
                    lane == comps + my_trial * trials_here + k, trial_wide, 0.0
                ),
                axis=1,
                keepdims=True,
            )
            for k in range(trials_here)
        ]

        weights = jnp.concatenate(
            [(neuron_now * own[k]).astype(jnp.bfloat16) for k in range(trials_here)],
            axis=1,
        )
        columns = by_columns and sweep == SWEEPS - 1
        local = jnp.dot(weights, tensor_v[...], preferred_element_type=jnp.float32)
        if columns:
            for c in range(chunks):
                for g in range(groups):
                    tile = None
                    for h in range(groups):
                        part = local[
                            h * ROWS : (h + 1) * ROWS, c * LANES : (c + 1) * LANES
                        ]
                        if h != g:
                            part = pltpu.roll(part, ((h - g) * share) % LANES, 1)
                        tile = part if h == 0 else jnp.where(lane8 < h * share, tile, part)
                    time_local[c * groups + g] = tile

            def start_tile(slot, device):
                pltpu.make_async_remote_copy(
                    src_ref=time_local.at[device[0] * trial_devices + device[1]],
                    dst_ref=time_parts.at[slot],
                    send_sem=sends[2],
                    recv_sem=receives[2],
                    device_id=device,
                    device_id_type=MESH,
                ).start()

            each_other(start_tile)
        else:
            for t in range(trial_devices):
                share_local[sweep, t] = local[:, t * width : (t + 1) * width]

            def start_share(step):
                pltpu.make_async_remote_copy(
                    src_ref=share_local.at[sweep, trial_ids[step]],
                    dst_ref=share_parts.at[sweep, step],
                    send_sem=sends[2],
                    recv_sem=receives[2],
                    device_id=trial_peer(step),
                    device_id_type=MESH,
                ).start()

            each(1, trial_devices, start_share)
        trial_gram = split_gram(trial_wide)
        inverse = inverse_of(neuron_gram * trial_gram)
        wait_bytes(others, sends[1])

        if columns:
            others = time_parts.at[pl.ds(1, devices - 1)]
            wait_bytes(others, receives[2])
            tile = time_local[me] + jnp.sum(time_parts[1:devices], axis=0)
            mine = jnp.concatenate(
                [tile]
                + [pltpu.roll(tile, LANES - g * share, 1) for g in range(1, groups)],
                axis=0,
            )
            time_raw = apply_inverse(inverse, jnp.where(lane < share, mine, 0.0))
            sums = jnp.sum(time_raw * time_raw, axis=1, keepdims=True)
            norm_all[0] = jnp.sum(sums * eye, axis=0, keepdims=True)

            def start_norm(slot, device):
                pltpu.make_async_remote_copy(
                    src_ref=norm_all.at[0],
                    dst_ref=norm_all.at[slot],
                    send_sem=norm_sem.at[0],
                    recv_sem=norm_sem.at[1],
                    device_id=device,
                    device_id_type=MESH,
                ).start()

            each_other(start_norm)
            neuron_out[...] = neuron_now
            for k in range(trials_here):
                trial_out[k : k + 1, :] = jnp.sum(
                    own[k] * eye[:, :comps], axis=0, keepdims=True
                )
            wait_bytes(others, sends[2])
            others = norm_all.at[pl.ds(1, devices - 1)]
            wait_bytes(others, norm_sem.at[1])
            sums = jnp.sum(
                jnp.sum(norm_all[...], axis=0) * eye, axis=1, keepdims=True
            )
            down = lax.rsqrt(sums * (1.0 / timepoints) + tiny_eps)
            time_out[...] = (time_raw * down)[:, :share]
            wait_bytes(others, norm_sem.at[0])
            break

        others = share_parts.at[sweep, pl.ds(1, trial_devices - 1)]
        wait_bytes(others, receives[2])
        total = share_local[sweep, my_trial]
        for t in range(1, trial_devices):
            total = total + share_parts[sweep, t]
        middle[sweep, 0] = total.astype(jnp.bfloat16)

        def start_middle(step):
            pltpu.make_async_remote_copy(
                src_ref=middle.at[sweep, 0],
                dst_ref=middle.at[sweep, step],
                send_sem=sends[3],
                recv_sem=receives[3],
                device_id=neuron_peer(step),
                device_id_type=MESH,
            ).start()

        each(1, neuron_devices, start_middle)
        wait_bytes(others, sends[2])
        others = middle.at[sweep, pl.ds(1, neuron_devices - 1)]
        wait_bytes(others, receives[3])
        share_sums[sweep, my_trial] = jnp.sum(
            middle[sweep].astype(jnp.float32), axis=0
        )
        mine = share_sums.at[sweep, my_trial]
        send_all(mine, mine, trial_devices, trial_peer, sends[4], receives[4])
        wait_bytes(others, sends[3])
        others = share_sums.at[sweep, pl.ds(0, trial_devices - 1)]
        wait_bytes(others, receives[4])
        time_terms = jnp.concatenate(
            [share_sums[sweep, t] for t in range(trial_devices)], axis=1
        )
        time_raw = apply_inverse(inverse, time_terms)
        wait_bytes(others, sends[4])
        down = lax.rsqrt(
            jnp.sum(time_raw * time_raw, axis=1, keepdims=True) * (1.0 / timepoints)
            + tiny_eps
        )
        time_now = time_raw * down
        time_rounded = time_now.astype(jnp.bfloat16)
        if sweep == SWEEPS - 1:
            for c in range(chunks):
                time_keep[c] = time_now[:, c * LANES : (c + 1) * LANES]
            shares = LANES // share
            chunk = time_keep[me // shares]
            shift = lax.rem(LANES - lax.rem(me, shares) * share, LANES)
            time_out[...] = pltpu.roll(chunk, shift, 1)[:, :share]
            neuron_out[...] = neuron_now
            for k in range(trials_here):
                trial_out[k : k + 1, :] = jnp.sum(
                    own[k] * eye[:, :comps], axis=0, keepdims=True
                )


def keep(neuron_in, time_in, trial_in, neuron_out, time_out, trial_out, sem):
    copies = [
        pltpu.make_async_copy(neuron_in, neuron_out, sem.at[0]),
        pltpu.make_async_copy(time_in, time_out, sem.at[1]),
        pltpu.make_async_copy(trial_in, trial_out, sem.at[2]),
    ]
    for copy in copies:
        copy.start()
    for copy in copies:
        copy.wait()


def per_device(neuron_devices, trial_devices, tensor, time_init, trial_init):
    trials_here, neurons_here, timepoints = tensor.shape
    comps = time_init.shape[0]
    devices = neuron_devices * trial_devices
    tiles = (timepoints // LANES) * (comps // ROWS)
    shares = (SWEEPS, trial_devices, comps, timepoints // trial_devices)
    f32 = jnp.float32
    vmem = pl.BlockSpec(memory_space=pltpu.VMEM)
    results = pl.pallas_call(
        functools.partial(kernel, neuron_devices, trial_devices),
        out_shape=(
            jax.ShapeDtypeStruct((comps, neurons_here), f32),
            jax.ShapeDtypeStruct((comps, timepoints // devices), f32),
            jax.ShapeDtypeStruct((trials_here, comps), f32),
        ),
        in_specs=[pl.BlockSpec(memory_space=pl.ANY)] * 3,
        out_specs=(vmem, vmem, vmem),
        scratch_shapes=[
            pltpu.VMEM((trials_here * neurons_here, timepoints), jnp.bfloat16),
            pltpu.VMEM((comps, timepoints), f32),
            pltpu.VMEM((trials_here, comps), f32),
            pltpu.VMEM((trial_devices, comps, LANES), f32),
            pltpu.VMEM((SWEEPS, trial_devices, trials_here, comps, neurons_here), f32),
            pltpu.VMEM((SWEEPS, neuron_devices, comps // 2, LANES), f32),
            pltpu.VMEM((tiles, ROWS, LANES), f32),
            pltpu.VMEM((devices, ROWS, LANES), f32),
            pltpu.VMEM(shares, f32),
            pltpu.VMEM(shares, f32),
            pltpu.VMEM((SWEEPS, neuron_devices) + shares[2:], jnp.bfloat16),
            pltpu.VMEM(shares, f32),
            pltpu.VMEM((timepoints // LANES, comps, LANES), f32),
            pltpu.VMEM((devices, 1, LANES), f32),
            pltpu.SemaphoreType.DMA((2 + trials_here,)),
            pltpu.SemaphoreType.DMA((2,)),
            pltpu.SemaphoreType.DMA((2,)),
            pltpu.SemaphoreType.DMA((SWEEPS, 5)),
            pltpu.SemaphoreType.DMA((SWEEPS, 5)),
        ],
        compiler_params=pltpu.CompilerParams(
            collective_id=0,
            has_side_effects=True,
            vmem_limit_bytes=56 * 1024 * 1024,
        ),
    )(tensor, time_init, trial_init.T)
    neuron_now, time_now, trial_now = pl.pallas_call(
        keep,
        out_shape=tuple(jax.ShapeDtypeStruct(r.shape, f32) for r in results),
        in_specs=[pl.BlockSpec(memory_space=pl.ANY)] * 3,
        out_specs=(pl.BlockSpec(memory_space=pl.ANY),) * 3,
        scratch_shapes=[pltpu.SemaphoreType.DMA((3,))],
    )(*results)
    return neuron_now, time_now, trial_now.T


def solution(mesh):
    placed = (P("trial", "neuron", None), P(), P(None, "trial"))
    return jax.shard_map(
        functools.partial(per_device, mesh.shape["neuron"], mesh.shape["trial"]),
        mesh=mesh,
        in_specs=placed,
        out_specs=(P(None, "neuron"), P(None, ("neuron", "trial")), P(None, "trial")),
        check_vma=False,
    )
```
